128 devices in a mesh: chan: 16 (over z, x_hi, core), width: 8 (over y, x_lo).
Axes of the slice: x: 4 (x_hi: 2, x_lo: 2; x = x_hi * 2 + x_lo), y: 4, z: 4, core: 2. Of those that a mesh axis runs over, the one named last changes fastest.
Arguments:
- populations: float32 [19, 256, 128, 128], P(None, 'chan', 'width'), as said below
- moment_rates: float32 [15], replicated, may hold values from 0.8 to 1.9
- solid_flags: int32 [256, 128, 128], P('chan', 'width'), may hold values 0 or 1
- destination: int32 [524288, 1], P(('chan', 'width')), may hold values from 0 to 127; in each aligned block of 4096 rows (0 to 4095, 4096 to 8191, ...) at most 64 rows name the same one
- local_cell: int32 [524288], P(('chan', 'width')), may hold values from 0 to 32767
- particle_velocity: float32 [3, 524288], P(None, ('chan', 'width')), may hold values from -4 to 4
- coupling: float32 [524288], P(('chan', 'width')), may hold values from 0.05 to 0.5
Outputs:
- new_populations: float32 [19, 256, 128, 128], P(None, 'chan', 'width')
- new_particle_vel: float32 [3, 524288], P(None, ('chan', 'width'))
The draws below stay inside these ranges and needn't reach their ends.
Inputs may be any that keep to these rules, and one draw needn't show every extreme that they name: `destination`: the particles held by one device name each device at most 64 times, and in every draw some device names some device exactly 64 times. `populations`: each entry is its direction's lattice weight times a factor between 0.1 and 1.9.
All inputs are finite; a program needn't handle non-finite values. No bound on the sum of `solid_flags` on one device may be relied on, other than what follows from the above.
Results may differ from the reference program's by a relative error of at most 0.0001.
Values sent between devices are 32-bit elements; how exact they have to be, the bound alone decides.
A program may use at most 128 MiB of HBM per device.

```python
import math
import jax
import jax.numpy as jnp
import numpy as np
from jax import lax

CX = 16
CY = 16
NZ = 128
P_DEV = 4096
STEPS = 4
NX = 256
NY = 128
P_TOTAL = 524288
CAP = 64
N_CHAN = 16
N_WIDTH = 8


def draw_populations(key, part):
    key = jax.random.fold_in(key, 11)
    weights = jnp.array([1.0 / 3.0] + [1.0 / 18.0] * 6 + [1.0 / 36.0] * 12, dtype=jnp.float32)
    factor = jnp.clip(0.3 * jax.random.normal(key, (19, NX, NY, NZ), jnp.float32), -0.9, 0.9)
    return weights[:, None, None, None] * (1.0 + factor)


def touch_ends(values, stream_key, low, largest):
    dims = values.shape
    index_at = [jax.random.randint(jax.random.fold_in(stream_key, axis), (), 0, dims[axis]) for axis in range(len(dims))]
    values = values.at[tuple(index_at)].set(low)
    longest = dims.index(max(dims))
    index_at[longest] = (index_at[longest] + 1) % dims[longest]
    return values.at[tuple(index_at)].set(largest)


def steps_of(rng, extent, cuts, smallest, high):
    def one(position, parts):
        heights = jax.random.uniform(jax.random.fold_in(jax.random.fold_in(rng, 6), position), (parts,), jnp.float32, smallest / len(cuts), high / len(cuts))
        return jnp.repeat(jnp.exp(heights), extent[position] // parts).reshape((-1,) + (1,) * (len(extent) - position - 1))

    factor_of = one(*cuts[0])
    for cut in cuts[1:]:
        factor_of = factor_of * one(*cut)
    return factor_of


def deal_out(own_key, own, number, rows, number_of, top, most, slope):
    sequence = jax.random.permutation(own_key, number_of)
    packed, common = shares(number_of, rows * top, most, slope, True), shares(number_of, rows * top, most, slope, False)
    places = jnp.arange(number_of)

    def named(tallies, offset_by):
        used = int((tallies > 0).sum())
        fixed = max(1, used // 4)
        moved = fixed + (places - fixed + offset_by * (used - fixed)) % max(1, number_of - fixed)
        return jnp.zeros((number_of,), jnp.int32).at[sequence[jnp.where(places < fixed, places, moved)]].set(jnp.asarray(tallies, jnp.int32))

    tallies = jnp.where(number % 4 == 0, named(packed, number // 4), named(common, number - number // 4 - 1))
    mixed = jax.random.permutation(jax.random.fold_in(own, 3), number_of)
    donor, receiver = mixed[0:number_of // 2 * 2:2], mixed[1:number_of // 2 * 2:2]
    room = jnp.minimum(tallies[donor] - 1, most - tallies[receiver]) // 2
    room = jnp.where((donor == sequence[0]) | (receiver == sequence[0]) | (tallies[receiver] == 0), 0, jnp.maximum(room, 0))
    moved = jax.random.randint(jax.random.fold_in(own, 4), (number_of // 2,), 0, 1 << 20) % (room + 1)
    tallies = tallies.at[donor].add(-moved).at[receiver].add(moved)
    members = jnp.searchsorted(jnp.cumsum(tallies), jnp.arange(rows * top), side="right").astype(jnp.int32)
    listing = members.reshape(top, rows).T
    listing = listing[jax.random.permutation(jax.random.fold_in(own, 1), rows)]
    offset_by = jax.random.randint(jax.random.fold_in(own, 2), (rows, 1), 0, top)
    return jnp.take_along_axis(listing, (jnp.arange(top)[None, :] + offset_by) % top, axis=1)


def shares(number_of, total, most, skew, full):
    loads = [(1 << 20) // math.isqrt(standing ** skew) + 1 for standing in range(1, number_of + 1)]
    largest = most if full else min(most, max(-(-total // number_of), total * loads[0] // sum(loads)))
    least = 1 if total - largest >= number_of - 1 else 0
    holding, rest = [largest] + [least] * (number_of - 1), total - largest - least * (number_of - 1)
    while rest > 0:
        candidates = [i for i in range(1, number_of) if holding[i] < largest] or [i for i in range(1, number_of) if holding[i] < most]
        pool, left = sum([loads[i] for i in candidates]), rest
        for i in candidates:
            extra = min(most - holding[i], max(1, left * loads[i] // pool), rest)
            holding[i] = holding[i] + extra
            rest = rest - extra
    return np.array(holding)


def bell_draw(key, shape, spread, reach, cuts=(), kind=jnp.bfloat16):
    entries = jax.random.normal(key, shape, jnp.float32) * spread
    if len(cuts) > 0:
        entries = steps_of(key, shape, cuts, -0.22, 0.18) * entries
    return jnp.clip(entries, min=-reach, max=reach).astype(kind)


def setup_inputs(seed: int = 0) -> dict:
    key_list = jax.random.split(jax.random.key(seed), 8)
    populations = draw_populations(jax.random.fold_in(key_list[7], 71), 0)
    moment_rates = jnp.clip(jnp.exp(jax.random.uniform(key_list[1], (15,), jnp.float32, math.log(0.8), math.log(1.9))), 0.8, 1.9)
    solid_flags = touch_ends((jax.random.randint(key_list[2], (NX, NY, NZ), 0, 8) < 1).astype(jnp.int32), jax.random.fold_in(key_list[2], 1), 0, 1)
    destination_keys = jax.random.split(jax.random.fold_in(key_list[3], 1), P_TOTAL // P_DEV)
    destination_turns = jax.random.permutation(jax.random.fold_in(key_list[3], 3), P_TOTAL // P_DEV)
    destination = jax.vmap(lambda own, number: deal_out(jax.random.fold_in(key_list[3], 2), own, number, P_DEV, N_CHAN * N_WIDTH, 1, CAP, 2))(destination_keys, destination_turns).reshape((P_TOTAL, 1))
    local_cell = touch_ends(jax.random.randint(key_list[4], (P_TOTAL,), 0, CX * CY * NZ), jax.random.fold_in(key_list[4], 1), 0, (CX * CY * NZ) - 1).astype(jnp.int32)
    particle_velocity = bell_draw(key_list[5], (3, P_TOTAL), 1.0, 4.0, ((1, 128),), jnp.float32)
    coupling = jnp.clip(jnp.exp(math.log(0.5) - 2.3025851 * jax.random.uniform(key_list[6], (P_TOTAL,), jnp.float32) ** steps_of(key_list[6], (P_TOTAL,), ((0, 128),), -0.2, 0.2)), 0.05, 0.5)
    return {"populations": populations, "moment_rates": moment_rates, "solid_flags": solid_flags, "destination": destination, "local_cell": local_cell, "particle_velocity": particle_velocity, "coupling": coupling}


LATTICE = [[0, 0, 0], [1, 0, 0], [-1, 0, 0], [0, 1, 0], [0, -1, 0], [0, 0, 1], [0, 0, -1], [1, 1, 0], [-1, -1, 0], [1, -1, 0], [-1, 1, 0], [1, 0, 1], [-1, 0, -1], [1, 0, -1], [-1, 0, 1], [0, 1, 1], [0, -1, -1], [0, 1, -1], [0, -1, 1]]
OPPOSITE = [0, 2, 1, 4, 3, 6, 5, 8, 7, 10, 9, 12, 11, 14, 13, 16, 15, 18, 17]
LATTICE_WEIGHTS = [1.0 / 3.0] + [1.0 / 18.0] * 6 + [1.0 / 36.0] * 12
coupling_mass = 0.02

def moment_basis():
    lattice_np = np.array(LATTICE, dtype=np.float32)
    along_x, along_y, along_z = (lattice_np[:, 0], lattice_np[:, 1], lattice_np[:, 2])
    columns = [np.ones(19, dtype=np.float32), along_x, along_y, along_z, along_x * along_x, along_y * along_y, along_z * along_z, along_x * along_y, along_x * along_z, along_y * along_z, along_x * along_y * along_y, along_x * along_z * along_z, along_y * along_x * along_x, along_y * along_z * along_z, along_z * along_x * along_x, along_z * along_y * along_y, along_x * along_x * along_y * along_y, along_x * along_x * along_z * along_z, along_y * along_y * along_z * along_z]
    found_cols = []
    for column in columns:
        vector = np.array(column, dtype=np.float32)
        for repeat_pass in range(2):
            for earlier in found_cols:
                vector = vector - float(np.dot(earlier, vector)) * earlier
        found_cols.append((vector / math.sqrt(float(np.dot(vector, vector)))).astype(np.float32))
    return np.stack(found_cols[4:], axis=1).astype(np.float32)

def build_relax(moment_rates):
    basis = jnp.asarray(moment_basis())
    return jnp.dot(basis * moment_rates[None, :], basis.T, precision=lax.Precision.HIGHEST)

def lattice_tables():
    lattice_vel = jnp.asarray(np.array(LATTICE, dtype=np.float32))
    weights = jnp.asarray(np.array(LATTICE_WEIGHTS, dtype=np.float32))[:, None]
    return (lattice_vel, weights)

def moments(flat_pop):
    lattice_vel, weights = lattice_tables()
    density = lax.optimization_barrier(jnp.sum(flat_pop, axis=0))
    momentum = jnp.dot(lattice_vel.T, flat_pop, precision=lax.Precision.HIGHEST)
    return (density, momentum)

def relax_cells(flat_pop, density, momentum, cell_force, relaxation, solid_flat):
    lattice_vel, weights = lattice_tables()
    velocity = momentum + 0.5 * cell_force
    proj_vel = jnp.dot(lattice_vel, velocity, precision=lax.Precision.HIGHEST)
    proj_force = jnp.dot(lattice_vel, cell_force, precision=lax.Precision.HIGHEST)
    speed_sq = lax.optimization_barrier(jnp.sum(velocity * velocity, axis=0))
    work_dot = lax.optimization_barrier(jnp.sum(velocity * cell_force, axis=0))
    equilib = weights * (density + 3.0 * proj_vel + 4.5 * proj_vel * proj_vel - 1.5 * speed_sq)
    source = weights * (3.0 * (proj_force - work_dot) + 9.0 * proj_vel * proj_force)
    relaxed = flat_pop + source + jnp.dot(relaxation, equilib - flat_pop - 0.5 * source, precision=lax.Precision.HIGHEST)
    bounced = flat_pop[jnp.array(OPPOSITE, dtype=jnp.int32)]
    return jnp.where(solid_flat[None, :] == 1, bounced, relaxed)

def stream_global(relaxed):
    shifted = [jnp.roll(relaxed[k], shift=tuple(LATTICE[k]), axis=(0, 1, 2)) for k in range(19)]
    return jnp.stack(shifted)

def reference(populations, moment_rates, solid_flags, destination, local_cell, particle_velocity, coupling):
    relaxation = build_relax(moment_rates)
    owner_dev = destination[:, 0].astype(jnp.int32)
    chan_index = owner_dev // N_WIDTH
    width_index = owner_dev % N_WIDTH
    cell_x = local_cell // (CY * NZ)
    cell_y = local_cell // NZ % CY
    cell_z = local_cell % NZ
    global_cell = (((chan_index * CX + cell_x) * NY + width_index * CY + cell_y) * NZ + cell_z).astype(jnp.int32)
    solid_flat = solid_flags.reshape(-1)
    velocities = particle_velocity
    current = populations
    for iteration in range(STEPS):
        flat_pop = current.reshape(19, -1)
        density, momentum = moments(flat_pop)
        slip_vel = momentum[:, global_cell] - velocities
        momentum_kick = coupling[None, :] * slip_vel
        velocities = velocities + momentum_kick
        cell_force = jnp.zeros_like(momentum).at[:, global_cell].add(-coupling_mass * momentum_kick)
        relaxed = relax_cells(flat_pop, density, momentum, cell_force, relaxation, solid_flat)
        current = stream_global(relaxed.reshape(19, NX, NY, NZ))
    return (current, velocities)
```

```python
import functools
import math

import jax
import jax.numpy as jnp
import numpy as np
from jax import lax
from jax.experimental import pallas as pl
from jax.experimental.pallas import tpu as pltpu
from jax.sharding import PartitionSpec as P

MESH = pl.DeviceIdType.MESH
STEPS = 4
CAP = 64
LATTICE = [
    [0, 0, 0],
    [1, 0, 0],
    [-1, 0, 0],
    [0, 1, 0],
    [0, -1, 0],
    [0, 0, 1],
    [0, 0, -1],
    [1, 1, 0],
    [-1, -1, 0],
    [1, -1, 0],
    [-1, 1, 0],
    [1, 0, 1],
    [-1, 0, -1],
    [1, 0, -1],
    [-1, 0, 1],
    [0, 1, 1],
    [0, -1, -1],
    [0, 1, -1],
    [0, -1, 1],
]
OPPOSITE = [0, 2, 1, 4, 3, 6, 5, 8, 7, 10, 9, 12, 11, 14, 13, 16, 15, 18, 17]
COUPLING_MASS = 0.02
RING = [9, 1, 11, 13, 7, 3, 15, 17, 10, 2, 12, 14, 8, 4, 16, 18]
SLOT_OF = {k: i for i, k in enumerate(RING)}
STAY = {0: 0, 5: 1, 6: 2}
PAD = 8
DIAGONALS = [(0, 1, 7), (0, 2, 11), (1, 2, 15)]


def moment_basis():
    lattice_np = np.array(LATTICE, dtype=np.float32)
    along_x, along_y, along_z = (lattice_np[:, 0], lattice_np[:, 1], lattice_np[:, 2])
    columns = [
        np.ones(19, dtype=np.float32),
        along_x,
        along_y,
        along_z,
        along_x * along_x,
        along_y * along_y,
        along_z * along_z,
        along_x * along_y,
        along_x * along_z,
        along_y * along_z,
        along_x * along_y * along_y,
        along_x * along_z * along_z,
        along_y * along_x * along_x,
        along_y * along_z * along_z,
        along_z * along_x * along_x,
        along_z * along_y * along_y,
        along_x * along_x * along_y * along_y,
        along_x * along_x * along_z * along_z,
        along_y * along_y * along_z * along_z,
    ]
    found_cols = []
    for column in columns:
        vector = np.array(column, dtype=np.float32)
        for repeat_pass in range(2):
            for earlier in found_cols:
                vector = vector - float(np.dot(earlier, vector)) * earlier
        found_cols.append((vector / math.sqrt(float(np.dot(vector, vector)))).astype(np.float32))
    return np.stack(found_cols[4:], axis=1).astype(np.float32)


def sector_tables():
    basis = moment_basis().astype(np.float64)

    def vec(entries):
        v = np.zeros(19)
        for k, s in entries:
            v[k] = s
        return v

    def project(members):
        m = np.stack(members)
        dots = m @ basis
        dots[np.abs(dots) < 1e-5] = 0.0
        sizes = np.sum(np.abs(m), axis=1)
        return dots[:, None, :] * dots[None, :, :] / sizes[None, :, None]

    even = [vec([(0, 1)])]
    for a in range(3):
        even.append(vec([(1 + 2 * a, 1), (2 + 2 * a, 1)]))
    for a, b, k in DIAGONALS:
        even.append(vec([(k + i, 1) for i in range(4)]))
    table = project(even)
    table = table[1:, 1:] - table[1:, :1]
    table[:3] *= 0.5
    table[3:] *= 0.25
    even_table = table
    odd_tables = []
    for a in range(3):
        members = [vec([(1 + 2 * a, 1), (2 + 2 * a, -1)])]
        for p, q, k in DIAGONALS:
            if a in (p, q):
                members.append(vec([(k + i, LATTICE[k + i][a]) for i in range(4)]))
        table = project(members)
        odd_tables.append((table[1:, 1:] - table[1:, :1]) * 0.25)
    cross = []
    for p, q, k in DIAGONALS:
        table = project([vec([(k + i, LATTICE[k + i][p] * LATTICE[k + i][q]) for i in range(4)])])
        cross.append(table[0, 0] * 0.25)
    return even_table, odd_tables, cross


def weigh(rates, weights):
    total = None
    for j in range(15):
        if abs(weights[j]) > 1e-9:
            term = rates[j] * float(weights[j])
            total = term if total is None else total + term
    return total if total is not None else rates[0] * 0.0


def split_bf16(x):
    hi = x.astype(jnp.bfloat16)
    lo = (x - hi.astype(jnp.float32)).astype(jnp.bfloat16)
    return hi, lo


def dot_nt(a, b):
    return lax.dot_general(a, b, (((1,), (1,)), ((), ())), preferred_element_type=jnp.float32)


def dot_nn(a, b):
    return lax.dot_general(a, b, (((1,), (0,)), ((), ())), preferred_element_type=jnp.float32)


def relax_group(f, fields, seen_m, solid, coef):
    even_c, odd_c, cross_c = coef
    sums, diffs = [], []
    for a in range(3):
        p, n = f[1 + 2 * a], f[2 + 2 * a]
        sums.append(p + n)
        diffs.append(p - n)
    diag_sum, diag_cross, diag_first, diag_second = [], [], [], []
    for p, q, k in DIAGONALS:
        a1, b1 = f[k] + f[k + 1], f[k] - f[k + 1]
        a2, b2 = f[k + 2] + f[k + 3], f[k + 2] - f[k + 3]
        diag_sum.append(a1 + a2)
        diag_cross.append(a1 - a2)
        diag_first.append(b1 + b2)
        diag_second.append(b1 - b2)
    odd = [[], [], []]
    for g, (p, q, k) in enumerate(DIAGONALS):
        odd[p].append(diag_first[g])
        odd[q].append(diag_second[g])
    mom = [diffs[a] + (odd[a][0] + odd[a][1]) for a in range(3)]
    density = f[0] + ((sums[0] + sums[1]) + sums[2]) + ((diag_sum[0] + diag_sum[1]) + diag_sum[2])
    count, held, memory = fields
    force = []
    for a in range(3):
        kept = held[a]
        for weight, earlier in zip(memory, seen_m):
            kept = kept + weight * earlier[a]
        force.append(COUPLING_MASS * (kept - count * mom[a]))
    half = [0.5 * force[a] for a in range(3)]
    vel = [mom[a] + half[a] for a in range(3)]
    press = [mom[a] * mom[a] - half[a] * half[a] for a in range(3)]
    press_sum = press[0] + press[1] + press[2]
    work = [vel[a] * force[a] for a in range(3)]
    work_third = (work[0] + work[1] + work[2]) * (1.0 / 3.0)
    base = density * (1.0 / 9.0) - press_sum * (1.0 / 6.0)
    gaps = []
    for a in range(3):
        gaps.append(base + 0.5 * press[a] - sums[a])
    for g, (p, q, k) in enumerate(DIAGONALS):
        gaps.append(base + 0.5 * (press[p] + press[q]) - diag_sum[g])
    change = []
    for a in range(6):
        total = even_c[a][0] * gaps[0]
        for b in range(1, 6):
            total = total + even_c[a][b] * gaps[b]
        if a < 3:
            total = total + 0.5 * (work[a] - work_third)
        else:
            p, q, k = DIAGONALS[a - 3]
            total = total + 0.25 * (work[p] + work[q] - work_third)
        change.append(total)
    rest = f[0] - 2.0 * (change[0] + change[1] + change[2]) - 4.0 * (change[3] + change[4] + change[5])
    odd_axis, odd_diag = [], []
    for a in range(3):
        third = mom[a] * (1.0 / 3.0)
        g1, g2 = third - odd[a][0], third - odd[a][1]
        d1 = odd_c[a][0][0] * g1 + odd_c[a][0][1] * g2
        d2 = odd_c[a][1][0] * g1 + odd_c[a][1][1] * g2
        push = force[a] * (1.0 / 12.0)
        odd_axis.append(2.0 * (push - (d1 + d2)))
        odd_diag.append([push + d1, push + d2])
    out = [None] * 19
    out[0] = rest
    for a in range(3):
        out[1 + 2 * a] = f[1 + 2 * a] + (change[a] + odd_axis[a])
        out[2 + 2 * a] = f[2 + 2 * a] + (change[a] - odd_axis[a])
    place = [0, 0, 0]
    for g, (p, q, k) in enumerate(DIAGONALS):
        o1, o2 = odd_diag[p][place[p]], odd_diag[q][place[q]]
        place[p] += 1
        place[q] += 1
        gap = mom[p] * mom[q] - half[p] * half[q] - diag_cross[g]
        cross = cross_c[g] * gap + 0.25 * (vel[p] * force[q] + vel[q] * force[p])
        s_plus, s_minus = change[3 + g] + cross, change[3 + g] - cross
        o_plus, o_minus = o1 + o2, o1 - o2
        out[k] = f[k] + (s_plus + o_plus)
        out[k + 1] = f[k + 1] + (s_plus - o_plus)
        out[k + 2] = f[k + 2] + (s_minus + o_minus)
        out[k + 3] = f[k + 3] + (s_minus - o_minus)
    out = [jnp.where(solid, f[OPPOSITE[k]], out[k]) for k in range(19)]
    return out, mom


def kernel(
    dims,
    pop_hbm,
    rates,
    solid_ref,
    dest_ref,
    cell_ref,
    vel_ref,
    coup_ref,
    out_hbm,
    vel_out,
    pop,
    outv,
    moved,
    stayed,
    own_hits,
    rank_rows,
    packing,
    send1,
    recv1,
    send2,
    recv2,
    slots,
    plane_hits,
    depth_hits,
    spread,
    summed,
    fields,
    mom,
    mom_t,
    coef_ref,
    pop_sem,
    out_sem,
    a2a_send,
    a2a_recv,
    halo_send,
    halo_recv,
):
    n_chan, n_width, size_x, size_y, size_z, parts = dims
    n_dev = n_chan * n_width
    rows = n_dev * CAP // 128
    planes = size_x * size_y
    chan, width = lax.axis_index("chan"), lax.axis_index("width")
    me = chan * n_width + width
    f32, bf16, i32 = jnp.float32, jnp.bfloat16, jnp.int32

    barrier = pltpu.get_barrier_semaphore()

    def greet(i, _):
        o = lax.rem(me + i, n_dev)
        pl.semaphore_signal(
            barrier, inc=1, device_id=(o // n_width, lax.rem(o, n_width)), device_id_type=MESH
        )
        return 0

    lax.fori_loop(1, n_dev, greet, 0)
    pop_copy = pltpu.make_async_copy(pop_hbm, pop, pop_sem)
    pop_copy.start()

    even_table, odd_tables, cross_table = sector_tables()
    places = 0
    for a in range(6):
        for b in range(6):
            coef_ref[places] = weigh(rates, even_table[a, b])
            places += 1
    for axis in range(3):
        for a in range(2):
            for b in range(2):
                coef_ref[places] = weigh(rates, odd_tables[axis][a, b])
                places += 1
    for g in range(3):
        coef_ref[places] = weigh(rates, cross_table[g])
        places += 1

    block = 256
    tri = (
        lax.broadcasted_iota(i32, (block, block), 0) <= lax.broadcasted_iota(i32, (block, block), 1)
    ).astype(f32).astype(bf16)
    dev_iota = lax.broadcasted_iota(i32, (n_dev, block), 0)
    cap_iota = lax.broadcasted_iota(i32, (CAP, block), 0).astype(f32)

    def pack(b, before):
        s = pl.ds(pl.multiple_of(b * block, block), block)
        hits = jnp.where(dev_iota == dest_ref[:, s], 1.0, 0.0)
        hits_b = hits.astype(bf16)
        own_hits[:, s] = hits_b
        upto = dot_nn(hits_b, tri)
        rank = jnp.sum(hits * (upto + before), axis=0, keepdims=True) - 1.0
        rank_rows[:, s] = rank
        rank_hit = cap_iota == rank
        cell = cell_ref[:, s]
        pieces = []
        for value in (coup_ref[:, s], vel_ref[0:1, s], vel_ref[1:2, s], vel_ref[2:3, s]):
            pieces.append(split_bf16(value))
        order = [pieces[0][0], pieces[1][0], pieces[0][1], pieces[1][1]]
        order += [pieces[2][0], pieces[3][0], pieces[2][1], pieces[3][1]]
        order = [piece.astype(f32) for piece in order]
        order += [(cell // 128).astype(f32), lax.rem(cell, 128).astype(f32)]
        for j, row in enumerate(order):
            packing[j * CAP : (j + 1) * CAP, s] = jnp.where(rank_hit, row, 0.0).astype(bf16)
        return before + upto[:, block - 1 : block]

    lax.fori_loop(0, parts // block, pack, jnp.zeros((n_dev, 1), f32))
    packed = dot_nt(own_hits[...], packing[...])
    low = lax.broadcasted_iota(i32, (n_dev, 128), 1) < 64
    send1[0] = packed[:, 0:128] + packed[:, 128:256]
    send1[1] = packed[:, 256:384] + packed[:, 384:512]
    last = packed[:, 512:640]
    send1[2] = jnp.where(low, last * 128.0 + pltpu.roll(last, 64, 1), 0.0)

    pl.semaphore_wait(barrier, n_dev - 1)

    def exchange_start(src, dst, which):
        def send(i, _):
            o = lax.rem(me + i, n_dev)
            pltpu.make_async_remote_copy(
                src.at[:, pl.ds(o, 1)],
                dst.at[:, pl.ds(me, 1)],
                a2a_send.at[which],
                a2a_recv.at[which],
                device_id=(o // n_width, lax.rem(o, n_width)),
                device_id_type=MESH,
            ).start()
            return 0

        lax.fori_loop(1, n_dev, send, 0)
        dst[:, pl.ds(me, 1), :] = src[:, pl.ds(me, 1), :]

    def exchange_wait(src, dst, which):
        part = pl.ds(0, n_dev - 1)
        pltpu.make_async_copy(dst.at[:, part], dst.at[:, part], a2a_recv.at[which]).wait()
        pltpu.make_async_copy(src.at[:, part], src.at[:, part], a2a_send.at[which]).wait()

    exchange_start(send1, recv1, 0)
    exchange_wait(send1, recv1, 0)

    half_dev = n_dev // 2
    low = lax.broadcasted_iota(i32, (half_dev, 128), 1) < 64

    def both(ref):
        first, second = ref[0:half_dev, :], ref[half_dev:n_dev, :]
        return (
            jnp.where(low, first, pltpu.roll(second, 64, 1)),
            jnp.where(low, pltpu.roll(first, 64, 1), second),
        )

    coup, vx = both(recv1[0])
    vy, vz = both(recv1[1])
    cell = both(recv1[2])[0].astype(i32)
    slots[0], slots[1], slots[2], slots[3] = coup, vx, vy, vz
    slots[4] = (cell // 128).astype(f32)
    slots[5] = lax.rem(cell, 128).astype(f32)
    slots[6], slots[7], slots[8] = coup * vx, coup * vy, coup * vz
    slots[9] = coup

    plane_iota = lax.broadcasted_iota(i32, (planes, 128), 0).astype(f32)
    depth_iota = lax.broadcasted_iota(i32, (size_z, 128), 0).astype(f32)

    def place(i, _):
        s = pl.ds(pl.multiple_of(i * 128, 128), 128)
        plane_hits[:, s] = jnp.where(plane_iota == slots[4, pl.ds(i, 1), :], 1.0, 0.0).astype(bf16)
        depth_hits[:, s] = jnp.where(depth_iota == slots[5, pl.ds(i, 1), :], 1.0, 0.0).astype(bf16)
        return 0

    lax.fori_loop(0, rows, place, 0)

    chunk = min(1024, rows * 128)
    chunk_rows = chunk // 128

    def scatter(targets):
        summed[...] = jnp.zeros_like(summed)

        def one(n, _):
            for r in range(chunk_rows):
                i = n * chunk_rows + r
                hits = depth_hits[:, pl.ds(pl.multiple_of(i * 128, 128), 128)]
                hits = hits.reshape(size_z // 16, 16, 128)
                for j in range(4):
                    value = jnp.broadcast_to(slots[6 + j, pl.ds(i, 1), :], (16, 128))
                    for h, piece in enumerate(split_bf16(value)):
                        at = (2 * j + h) * size_z
                        spread[at : at + size_z, r * 128 : (r + 1) * 128] = (
                            hits * piece[None]
                        ).reshape(size_z, 128)
            s = pl.ds(pl.multiple_of(n * chunk, chunk), chunk)
            summed[...] += dot_nt(plane_hits[:, s], spread[...])
            return 0

        lax.fori_loop(0, rows // chunk_rows, one, 0)
        for j, target in enumerate(targets):
            at = 2 * j * size_z
            fields[target] = summed[:, at : at + size_z] + summed[:, at + size_z : at + 2 * size_z]

    def gather(t):
        for a in range(3):
            hi, lo = split_bf16(mom[t, a].T)
            mom_t[a * size_z : (a + 1) * size_z, :] = hi
            mom_t[(3 + a) * size_z : (4 + a) * size_z, :] = lo

        def one(n, _):
            s = pl.ds(pl.multiple_of(n * 256, 256), 256)
            found = dot_nn(mom_t[...], plane_hits[:, s])
            for r in range(2):
                i = 2 * n + r
                hit = depth_iota == slots[5, pl.ds(i, 1), :]
                c = slots[0, pl.ds(i, 1), :]
                lanes = slice(r * 128, (r + 1) * 128)
                for a in range(3):
                    both = (
                        found[a * size_z : (a + 1) * size_z, lanes]
                        + found[(3 + a) * size_z : (4 + a) * size_z, lanes]
                    )
                    seen = jnp.sum(jnp.where(hit, both, 0.0), axis=0, keepdims=True)
                    v = slots[1 + a, pl.ds(i, 1), :]
                    slots[1 + a, pl.ds(i, 1), :] = v + c * (seen - v)
            return 0

        lax.fori_loop(0, rows // 2, one, 0)

    def nb(dc, dw):
        return (lax.rem(chan + dc + n_chan, n_chan), lax.rem(width + dw + n_width, n_width))

    inner_x, inner_y = pl.ds(1, size_x), pl.ds(PAD, size_y)
    last_x, last_y = size_x, PAD + size_y - 1
    end_x, end_y = size_x + 1, PAD + size_y

    def halo_copies(t):
        g = moved.at[t % 2]
        parts_list = [
            (g.at[0:5, last_x, inner_y], g.at[0:5, 0, inner_y], nb(1, 0)),
            (g.at[8:13, 1, inner_y], g.at[8:13, end_x, inner_y], nb(-1, 0)),
            (g.at[4:9, inner_x, last_y], g.at[4:9, inner_x, PAD - 1], nb(0, 1)),
            (g.at[12:16, inner_x, PAD], g.at[12:16, inner_x, end_y], nb(0, -1)),
            (g.at[0:1, inner_x, PAD], g.at[0:1, inner_x, end_y], nb(0, -1)),
            (g.at[4, last_x, pl.ds(last_y, 1)], g.at[4, 0, pl.ds(PAD - 1, 1)], nb(1, 1)),
            (g.at[12, 1, pl.ds(PAD, 1)], g.at[12, end_x, pl.ds(end_y, 1)], nb(-1, -1)),
            (g.at[0, last_x, pl.ds(PAD, 1)], g.at[0, 0, pl.ds(end_y, 1)], nb(1, -1)),
            (g.at[8, 1, pl.ds(last_y, 1)], g.at[8, end_x, pl.ds(PAD - 1, 1)], nb(-1, 1)),
        ]
        return [
            pltpu.make_async_remote_copy(
                src, dst, halo_send.at[t, n], halo_recv.at[t, n], device_id=to, device_id_type=MESH
            )
            for n, (src, dst, to) in enumerate(parts_list)
        ]

    def load(t, i, h):
        f = []
        for k in range(19):
            if t == 0:
                f.append(pop[k, i, 8 * h : 8 * h + 8, :])
            elif k in STAY:
                f.append(stayed[(t - 1) % 2, STAY[k], i, 8 * h : 8 * h + 8, :])
            else:
                step_x, step_y, _ = LATTICE[k]
                start = PAD + 8 * h - step_y
                f.append(moved[(t - 1) % 2, SLOT_OF[k], i + 1 - step_x, start : start + 8, :])
        return f

    def step(t):
        def one(i, _):
            coef = [coef_ref[n] for n in range(51)]
            even_c = [coef[6 * a : 6 * a + 6] for a in range(6)]
            odd_c = [
                [coef[36 + 4 * a : 38 + 4 * a], coef[38 + 4 * a : 40 + 4 * a]] for a in range(3)
            ]
            coefs = (even_c, odd_c, coef[48:51])
            for h in range(size_y // 8):
                f = load(t, i, h)
                at = pl.ds(pl.multiple_of(i * size_y + 8 * h, 8), 8)
                count = fields[0, at, :]
                held = [fields[1 + a, at, :] for a in range(3)]
                memory = [fields[4 + t - 1 - s, at, :] for s in range(t)]
                seen_m = [[mom[s, a, at, :] for a in range(3)] for s in range(t)]
                solid = solid_ref[i, 8 * h : 8 * h + 8, :] == 1
                out, m = relax_group(f, (count, held, memory), seen_m, solid, coefs)
                for a in range(3):
                    mom[t, a, at, :] = m[a]
                for k in range(19):
                    value = out[k]
                    if LATTICE[k][2]:
                        value = pltpu.roll(value, LATTICE[k][2] % size_z, 1)
                    if k in STAY:
                        stayed[t % 2, STAY[k], i, 8 * h : 8 * h + 8, :] = value
                    else:
                        moved[t % 2, SLOT_OF[k], i + 1, PAD + 8 * h : PAD + 8 * h + 8, :] = value
            return 0

        lax.fori_loop(0, size_x, one, 0)

    scatter([1, 2, 3, 0])
    coup = slots[0]
    keep = 1.0 - coup
    slots[9] = coup * coup
    pop_copy.wait()
    for t in range(STEPS):
        step(t)
        copies = halo_copies(t)
        for copy in copies:
            copy.start()
        gather(t)
        if t < STEPS - 1:
            for a in range(3):
                slots[6 + a] = slots[6 + a] * keep
            if t > 0:
                slots[9] = slots[9] * keep
            scatter([1, 2, 3, 4 + t])
        else:
            low = lax.broadcasted_iota(i32, (half_dev, 128), 1) < 64
            vx, vy, vz = slots[1], slots[2], slots[3]
            send2[0, 0:half_dev, :] = jnp.where(low, vx, pltpu.roll(vy, 64, 1))
            send2[0, half_dev:n_dev, :] = jnp.where(low, pltpu.roll(vx, 64, 1), vy)
            send2[1, 0:half_dev, :] = jnp.where(low, vz, 0.0)
            send2[1, half_dev:n_dev, :] = jnp.where(low, pltpu.roll(vz, 64, 1), 0.0)
            exchange_start(send2, recv2, 1)
        for copy in copies:
            copy.wait()

    def finish(i, _):
        for h in range(size_y // 8):
            f = load(STEPS, i, h)
            for k in range(19):
                outv[k, i, 8 * h : 8 * h + 8, :] = f[k]
        return 0

    lax.fori_loop(0, size_x, finish, 0)
    out_copy = pltpu.make_async_copy(outv, out_hbm, out_sem)
    out_copy.start()
    exchange_wait(send2, recv2, 1)

    back = [split_bf16(recv2[a].T) for a in range(2)]
    back = jnp.concatenate(
        [back[0][0], back[1][0][0:64], back[0][1], back[1][1][0:64]], axis=0
    )

    def unpack(b, _):
        s = pl.ds(pl.multiple_of(b * block, block), block)
        found = dot_nn(back, own_hits[:, s])
        hit = cap_iota == rank_rows[:, s]
        for a in range(3):
            value = found[64 * a : 64 * a + 64] + found[64 * (a + 3) : 64 * (a + 3) + 64]
            vel_out[a : a + 1, s] = jnp.sum(jnp.where(hit, value, 0.0), axis=0, keepdims=True)
        return 0

    lax.fori_loop(0, parts // block, unpack, 0)
    out_copy.wait()


def per_device(
    n_chan,
    n_width,
    populations,
    moment_rates,
    solid_flags,
    destination,
    local_cell,
    particle_velocity,
    coupling,
):
    _, size_x, size_y, size_z = populations.shape
    parts = destination.shape[0]
    n_dev = n_chan * n_width
    rows = n_dev * CAP // 128
    planes = size_x * size_y
    f32, bf16 = jnp.float32, jnp.bfloat16
    vmem = pl.BlockSpec(memory_space=pltpu.VMEM)
    chunk = min(1024, rows * 128)
    return pl.pallas_call(
        functools.partial(kernel, (n_chan, n_width, size_x, size_y, size_z, parts)),
        out_shape=(
            jax.ShapeDtypeStruct(populations.shape, f32),
            jax.ShapeDtypeStruct(particle_velocity.shape, f32),
        ),
        in_specs=[
            pl.BlockSpec(memory_space=pl.ANY),
            pl.BlockSpec(memory_space=pltpu.SMEM),
            vmem,
            vmem,
            vmem,
            vmem,
            vmem,
        ],
        out_specs=(pl.BlockSpec(memory_space=pl.ANY), vmem),
        scratch_shapes=[
            pltpu.VMEM(populations.shape, f32),
            pltpu.VMEM(populations.shape, f32),
            pltpu.VMEM((2, 16, size_x + 2, size_y + 2 * PAD, size_z), f32),
            pltpu.VMEM((2, 3, size_x, size_y, size_z), f32),
            pltpu.VMEM((n_dev, parts), bf16),
            pltpu.VMEM((1, parts), f32),
            pltpu.VMEM((10 * CAP, parts), bf16),
            pltpu.VMEM((3, n_dev, 128), f32),
            pltpu.VMEM((3, n_dev, 128), f32),
            pltpu.VMEM((2, n_dev, 128), f32),
            pltpu.VMEM((2, n_dev, 128), f32),
            pltpu.VMEM((10, rows, 128), f32),
            pltpu.VMEM((planes, rows * 128), bf16),
            pltpu.VMEM((size_z, rows * 128), bf16),
            pltpu.VMEM((8 * size_z, chunk), bf16),
            pltpu.VMEM((planes, 8 * size_z), f32),
            pltpu.VMEM((7, planes, size_z), f32),
            pltpu.VMEM((STEPS, 3, planes, size_z), f32),
            pltpu.VMEM((6 * size_z, planes), bf16),
            pltpu.SMEM((64,), f32),
            pltpu.SemaphoreType.DMA,
            pltpu.SemaphoreType.DMA,
            pltpu.SemaphoreType.DMA((2,)),
            pltpu.SemaphoreType.DMA((2,)),
            pltpu.SemaphoreType.DMA((STEPS, 9)),
            pltpu.SemaphoreType.DMA((STEPS, 9)),
        ],
        compiler_params=pltpu.CompilerParams(
            collective_id=0, has_side_effects=True, vmem_limit_bytes=56 * 1024 * 1024
        ),
        name="lattice_steps",
    )(
        populations,
        moment_rates,
        solid_flags,
        destination.reshape(1, parts),
        local_cell.reshape(1, parts),
        particle_velocity,
        coupling.reshape(1, parts),
    )


def solution(mesh):
    return jax.shard_map(
        functools.partial(per_device, mesh.shape["chan"], mesh.shape["width"]),
        mesh=mesh,
        in_specs=(
            P(None, "chan", "width", None),
            P(),
            P("chan", "width", None),
            P(("chan", "width"), None),
            P(("chan", "width")),
            P(None, ("chan", "width")),
            P(("chan", "width")),
        ),
        out_specs=(P(None, "chan", "width", None), P(None, ("chan", "width"))),
        check_vma=False,
    )
```

```python
import functools
import math

import jax
import jax.numpy as jnp
import numpy as np
from jax import lax
from jax.experimental import pallas as pl
from jax.experimental.pallas import tpu as pltpu
from jax.sharding import PartitionSpec as P

MESH = pl.DeviceIdType.MESH
STEPS = 4
CAP = 64
LATTICE = [
    [0, 0, 0],
    [1, 0, 0],
    [-1, 0, 0],
    [0, 1, 0],
    [0, -1, 0],
    [0, 0, 1],
    [0, 0, -1],
    [1, 1, 0],
    [-1, -1, 0],
    [1, -1, 0],
    [-1, 1, 0],
    [1, 0, 1],
    [-1, 0, -1],
    [1, 0, -1],
    [-1, 0, 1],
    [0, 1, 1],
    [0, -1, -1],
    [0, 1, -1],
    [0, -1, 1],
]
OPPOSITE = [0, 2, 1, 4, 3, 6, 5, 8, 7, 10, 9, 12, 11, 14, 13, 16, 15, 18, 17]
COUPLING_MASS = 0.02
RING = [9, 1, 11, 13, 7, 3, 15, 17, 10, 2, 12, 14, 8, 4, 16, 18]
SLOT_OF = {k: i for i, k in enumerate(RING)}
STAY = {0: 0, 5: 1, 6: 2}
PAD = 8
DIAGONALS = [(0, 1, 7), (0, 2, 11), (1, 2, 15)]


def moment_basis():
    lattice_np = np.array(LATTICE, dtype=np.float32)
    along_x, along_y, along_z = (lattice_np[:, 0], lattice_np[:, 1], lattice_np[:, 2])
    columns = [
        np.ones(19, dtype=np.float32),
        along_x,
        along_y,
        along_z,
        along_x * along_x,
        along_y * along_y,
        along_z * along_z,
        along_x * along_y,
        along_x * along_z,
        along_y * along_z,
        along_x * along_y * along_y,
        along_x * along_z * along_z,
        along_y * along_x * along_x,
        along_y * along_z * along_z,
        along_z * along_x * along_x,
        along_z * along_y * along_y,
        along_x * along_x * along_y * along_y,
        along_x * along_x * along_z * along_z,
        along_y * along_y * along_z * along_z,
    ]
    found_cols = []
    for column in columns:
        vector = np.array(column, dtype=np.float32)
        for repeat_pass in range(2):
            for earlier in found_cols:
                vector = vector - float(np.dot(earlier, vector)) * earlier
        found_cols.append((vector / math.sqrt(float(np.dot(vector, vector)))).astype(np.float32))
    return np.stack(found_cols[4:], axis=1).astype(np.float32)


def sector_tables():
    basis = moment_basis().astype(np.float64)

    def vec(entries):
        v = np.zeros(19)
        for k, s in entries:
            v[k] = s
        return v

    def project(members):
        m = np.stack(members)
        dots = m @ basis
        dots[np.abs(dots) < 1e-5] = 0.0
        sizes = np.sum(np.abs(m), axis=1)
        return dots[:, None, :] * dots[None, :, :] / sizes[None, :, None]

    even = [vec([(0, 1)])]
    for a in range(3):
        even.append(vec([(1 + 2 * a, 1), (2 + 2 * a, 1)]))
    for a, b, k in DIAGONALS:
        even.append(vec([(k + i, 1) for i in range(4)]))
    table = project(even)
    table = table[1:, 1:] - table[1:, :1]
    table[:3] *= 0.5
    table[3:] *= 0.25
    even_table = table
    odd_tables = []
    for a in range(3):
        members = [vec([(1 + 2 * a, 1), (2 + 2 * a, -1)])]
        for p, q, k in DIAGONALS:
            if a in (p, q):
                members.append(vec([(k + i, LATTICE[k + i][a]) for i in range(4)]))
        table = project(members)
        odd_tables.append((table[1:, 1:] - table[1:, :1]) * 0.25)
    cross = []
    for p, q, k in DIAGONALS:
        table = project([vec([(k + i, LATTICE[k + i][p] * LATTICE[k + i][q]) for i in range(4)])])
        cross.append(table[0, 0] * 0.25)
    return even_table, odd_tables, cross


def weigh(rates, weights):
    total = None
    for j in range(15):
        if abs(weights[j]) > 1e-9:
            term = rates[j] * float(weights[j])
            total = term if total is None else total + term
    return total if total is not None else jnp.zeros_like(rates[0])


def split_bf16(x):
    hi = x.astype(jnp.bfloat16)
    lo = (x - hi.astype(jnp.float32)).astype(jnp.bfloat16)
    return hi, lo


def dot_nt(a, b):
    return lax.dot_general(a, b, (((1,), (1,)), ((), ())), preferred_element_type=jnp.float32)


def dot_nn(a, b):
    return lax.dot_general(a, b, (((1,), (0,)), ((), ())), preferred_element_type=jnp.float32)


def relax_group(f, fields, seen_m, solid, coef):
    even_c, odd_c, cross_c = coef
    sums, diffs = [], []
    for a in range(3):
        p, n = f[1 + 2 * a], f[2 + 2 * a]
        sums.append(p + n)
        diffs.append(p - n)
    diag_sum, diag_cross, diag_first, diag_second = [], [], [], []
    for p, q, k in DIAGONALS:
        a1, b1 = f[k] + f[k + 1], f[k] - f[k + 1]
        a2, b2 = f[k + 2] + f[k + 3], f[k + 2] - f[k + 3]
        diag_sum.append(a1 + a2)
        diag_cross.append(a1 - a2)
        diag_first.append(b1 + b2)
        diag_second.append(b1 - b2)
    odd = [[], [], []]
    for g, (p, q, k) in enumerate(DIAGONALS):
        odd[p].append(diag_first[g])
        odd[q].append(diag_second[g])
    mom = [diffs[a] + (odd[a][0] + odd[a][1]) for a in range(3)]
    density = f[0] + ((sums[0] + sums[1]) + sums[2]) + ((diag_sum[0] + diag_sum[1]) + diag_sum[2])
    count, held, memory = fields
    force = []
    for a in range(3):
        kept = held[a]
        for weight, earlier in zip(memory, seen_m):
            kept = kept + weight * earlier[a]
        force.append(COUPLING_MASS * (kept - count * mom[a]))
    half = [0.5 * force[a] for a in range(3)]
    vel = [mom[a] + half[a] for a in range(3)]
    press = [mom[a] * mom[a] - half[a] * half[a] for a in range(3)]
    press_sum = press[0] + press[1] + press[2]
    work = [vel[a] * force[a] for a in range(3)]
    work_third = (work[0] + work[1] + work[2]) * (1.0 / 3.0)
    base = density * (1.0 / 9.0) - press_sum * (1.0 / 6.0)
    gaps = []
    for a in range(3):
        gaps.append(base + 0.5 * press[a] - sums[a])
    for g, (p, q, k) in enumerate(DIAGONALS):
        gaps.append(base + 0.5 * (press[p] + press[q]) - diag_sum[g])
    change = []
    for a in range(6):
        total = even_c[a][0] * gaps[0]
        for b in range(1, 6):
            total = total + even_c[a][b] * gaps[b]
        if a < 3:
            total = total + 0.5 * (work[a] - work_third)
        else:
            p, q, k = DIAGONALS[a - 3]
            total = total + 0.25 * (work[p] + work[q] - work_third)
        change.append(total)
    rest = f[0] - 2.0 * (change[0] + change[1] + change[2]) - 4.0 * (change[3] + change[4] + change[5])
    odd_axis, odd_diag = [], []
    for a in range(3):
        third = mom[a] * (1.0 / 3.0)
        g1, g2 = third - odd[a][0], third - odd[a][1]
        d1 = odd_c[a][0][0] * g1 + odd_c[a][0][1] * g2
        d2 = odd_c[a][1][0] * g1 + odd_c[a][1][1] * g2
        push = force[a] * (1.0 / 12.0)
        odd_axis.append(2.0 * (push - (d1 + d2)))
        odd_diag.append([push + d1, push + d2])
    out = [None] * 19
    out[0] = rest
    for a in range(3):
        out[1 + 2 * a] = f[1 + 2 * a] + (change[a] + odd_axis[a])
        out[2 + 2 * a] = f[2 + 2 * a] + (change[a] - odd_axis[a])
    place = [0, 0, 0]
    for g, (p, q, k) in enumerate(DIAGONALS):
        o1, o2 = odd_diag[p][place[p]], odd_diag[q][place[q]]
        place[p] += 1
        place[q] += 1
        gap = mom[p] * mom[q] - half[p] * half[q] - diag_cross[g]
        cross = cross_c[g] * gap + 0.25 * (vel[p] * force[q] + vel[q] * force[p])
        s_plus, s_minus = change[3 + g] + cross, change[3 + g] - cross
        o_plus, o_minus = o1 + o2, o1 - o2
        out[k] = f[k] + (s_plus + o_plus)
        out[k + 1] = f[k + 1] + (s_plus - o_plus)
        out[k + 2] = f[k + 2] + (s_minus + o_minus)
        out[k + 3] = f[k + 3] + (s_minus - o_minus)
    out = [jnp.where(solid, f[OPPOSITE[k]], out[k]) for k in range(19)]
    return out, mom


def kernel(
    dims,
    pop_hbm,
    rates_ref,
    solid_ref,
    dest_ref,
    cell_ref,
    vel_ref,
    coup_ref,
    out_hbm,
    back_out,
    rank_rows,
    pop,
    moved,
    stayed,
    own_hits,
    packing,
    send1,
    recv1,
    send2,
    recv2,
    slots,
    cells,
    weights,
    seen,
    plane_hits,
    depth_hits,
    spread_a,
    spread_b,
    summed,
    found_a,
    found_b,
    fields,
    mom,
    mom_t,
    coef_ref,
    pop_sem,
    out_sem,
    a2a_send,
    a2a_recv,
    halo_send,
    halo_recv,
):
    n_chan, n_width, size_x, size_y, size_z, parts = dims
    n_dev = n_chan * n_width
    rows = n_dev * CAP // 128
    planes = size_x * size_y
    chan, width = lax.axis_index("chan"), lax.axis_index("width")
    me = chan * n_width + width
    f32, bf16, i32 = jnp.float32, jnp.bfloat16, jnp.int32

    barrier = pltpu.get_barrier_semaphore()

    def greet(i, _):
        o = lax.rem(me + i, n_dev)
        pl.semaphore_signal(
            barrier, inc=1, device_id=(o // n_width, lax.rem(o, n_width)), device_id_type=MESH
        )
        return 0

    lax.fori_loop(1, n_dev, greet, 0)
    pop_copy = pltpu.make_async_copy(pop_hbm, pop, pop_sem)
    pop_copy.start()

    even_table, odd_tables, cross_table = sector_tables()
    rates = [jnp.full((8, 128), rates_ref[j], f32) for j in range(15)]
    places = 0
    for a in range(6):
        for b in range(6):
            coef_ref[places] = weigh(rates, even_table[a, b])
            places += 1
    for axis in range(3):
        for a in range(2):
            for b in range(2):
                coef_ref[places] = weigh(rates, odd_tables[axis][a, b])
                places += 1
    for g in range(3):
        coef_ref[places] = weigh(rates, cross_table[g])
        places += 1

    block = 256
    tri = (
        lax.broadcasted_iota(i32, (block, block), 0) <= lax.broadcasted_iota(i32, (block, block), 1)
    ).astype(f32).astype(bf16)
    dev_iota = lax.broadcasted_iota(i32, (n_dev, block), 0)
    cap_iota = lax.broadcasted_iota(i32, (CAP, block), 0).astype(f32)

    def pack(b, before):
        s = pl.ds(pl.multiple_of(b * block, block), block)
        hits = jnp.where(dev_iota == dest_ref[:, s], 1.0, 0.0)
        hits_b = hits.astype(bf16)
        own_hits[:, s] = hits_b
        upto = dot_nn(hits_b, tri)
        rank = jnp.sum(hits * (upto + before), axis=0, keepdims=True) - 1.0
        rank_rows[:, s] = rank
        rank_hit = cap_iota == rank
        cell = cell_ref[:, s]
        pieces = []
        for value in (coup_ref[:, s], vel_ref[0:1, s], vel_ref[1:2, s], vel_ref[2:3, s]):
            pieces.append(split_bf16(value))
        order = [pieces[0][0], pieces[1][0], pieces[0][1], pieces[1][1]]
        order += [pieces[2][0], pieces[3][0], pieces[2][1], pieces[3][1]]
        order = [piece.astype(f32) for piece in order]
        order += [(cell // 128).astype(f32), lax.rem(cell, 128).astype(f32)]
        for j, row in enumerate(order):
            packing[j * CAP : (j + 1) * CAP, s] = jnp.where(rank_hit, row, 0.0).astype(bf16)
        return before + upto[:, block - 1 : block]

    lax.fori_loop(0, parts // block, pack, jnp.zeros((n_dev, 1), f32), unroll=4)
    packed = dot_nt(own_hits[...], packing[...])
    low = lax.broadcasted_iota(i32, (n_dev, 128), 1) < 64
    send1[0] = packed[:, 0:128] + packed[:, 128:256]
    send1[1] = packed[:, 256:384] + packed[:, 384:512]
    last = packed[:, 512:640]
    send1[2] = jnp.where(low, last * 128.0 + pltpu.roll(last, 64, 1), 0.0)

    pl.semaphore_wait(barrier, n_dev - 1)

    def exchange_send(src, dst, which, o):
        pltpu.make_async_remote_copy(
            src.at[:, pl.ds(o, 1)],
            dst.at[:, pl.ds(me, 1)],
            a2a_send.at[which],
            a2a_recv.at[which],
            device_id=(o // n_width, lax.rem(o, n_width)),
            device_id_type=MESH,
        ).start()

    def exchange_wait(src, dst, which):
        part = pl.ds(0, n_dev - 1)
        pltpu.make_async_copy(dst.at[:, part], dst.at[:, part], a2a_recv.at[which]).wait()
        pltpu.make_async_copy(src.at[:, part], src.at[:, part], a2a_send.at[which]).wait()

    def send_one(i, _):
        exchange_send(send1, recv1, 0, lax.rem(me + i, n_dev))
        return 0

    lax.fori_loop(1, n_dev, send_one, 0)
    recv1[:, pl.ds(me, 1), :] = send1[:, pl.ds(me, 1), :]
    exchange_wait(send1, recv1, 0)

    half_dev = n_dev // 2
    low = lax.broadcasted_iota(i32, (half_dev, 128), 1) < 64

    def both(ref):
        first, second = ref[0:half_dev, :], ref[half_dev:n_dev, :]
        return (
            jnp.where(low, first, pltpu.roll(second, 64, 1)),
            jnp.where(low, pltpu.roll(first, 64, 1), second),
        )

    coup, vx = both(recv1[0])
    vy, vz = both(recv1[1])
    cell = both(recv1[2])[0].astype(i32)
    slots[0], slots[1], slots[2], slots[3] = coup, vx, vy, vz
    cells[0] = (cell // 128).astype(f32)
    cells[1] = lax.rem(cell, 128).astype(f32)
    weights[0], weights[1], weights[2] = coup * vx, coup * vy, coup * vz
    weights[3] = coup

    plane_iota = lax.broadcasted_iota(i32, (planes, 128), 0).astype(f32)
    depth_iota = lax.broadcasted_iota(i32, (size_z, 128), 0).astype(f32)

    def place(i, _):
        s = pl.ds(pl.multiple_of(i * 128, 128), 128)
        hits = jnp.where(plane_iota == cells[0, pl.ds(i, 1), :], 1.0, 0.0).astype(bf16)
        plane_hits[0:planes, s] = hits
        plane_hits[planes : 2 * planes, s] = hits
        depth_hits[:, s] = jnp.where(depth_iota == cells[1, pl.ds(i, 1), :], 1.0, 0.0).astype(bf16)
        return 0

    lax.fori_loop(0, rows, place, 0, unroll=2)

    chunk = min(2048, rows * 128 // 2)
    chunk_rows = chunk // 128

    chunks = rows // chunk_rows

    def weigh_chunk(n, spread):
        for r in range(chunk_rows):
            i = n * chunk_rows + r
            hits = depth_hits[:, pl.ds(pl.multiple_of(i * 128, 128), 128)]
            hits = hits.reshape(size_z // 16, 16, 128)
            for j in range(4):
                value = jnp.broadcast_to(weights[j, pl.ds(i, 1), :], (16, 128))
                for h, piece in enumerate(split_bf16(value)):
                    at = (2 * j + h) * size_z
                    spread[at : at + size_z, r * 128 : (r + 1) * 128] = (
                        hits * piece[None]
                    ).reshape(size_z, 128)

    def add_chunk(n, spread):
        s = pl.ds(pl.multiple_of(n * chunk, chunk), chunk)
        summed[...] += dot_nt(spread[...], plane_hits[0:planes, s])

    def scatter(targets, beside=None):
        summed[...] = jnp.zeros_like(summed)
        weigh_chunk(0, spread_a)
        share = size_x // chunks

        def two(n, _):
            weigh_chunk(2 * n + 1, spread_b)
            add_chunk(2 * n, spread_a)
            if beside is not None:
                for i in range(share):
                    beside(2 * n * share + i)
            weigh_chunk(lax.rem(2 * n + 2, chunks), spread_a)
            add_chunk(2 * n + 1, spread_b)
            if beside is not None:
                for i in range(share):
                    beside((2 * n + 1) * share + i)
            return 0

        lax.fori_loop(0, chunks // 2, two, 0)
        for j, target in enumerate(targets):
            at = 2 * j * size_z
            total = summed[at : at + size_z, :] + summed[at + size_z : at + 2 * size_z, :]
            fields[target] = total.T

    tile = min(1024, rows * 128 // 2)
    tile_rows = tile // 128

    def find(n, found):
        s = pl.ds(pl.multiple_of(n * tile, tile), tile)
        found[...] = dot_nn(mom_t[...], plane_hits[:, s])

    def pick(n, found):
        for r in range(tile_rows):
            i = n * tile_rows + r
            hit = depth_iota == cells[1, pl.ds(i, 1), :]
            for a in range(3):
                both = found[a * size_z : (a + 1) * size_z, r * 128 : (r + 1) * 128]
                seen[a, pl.ds(i, 1), :] = jnp.sum(
                    jnp.where(hit, both, 0.0), axis=0, keepdims=True
                )

    tiles = rows // tile_rows
    first_tile = lax.rem(me, rows) // tile_rows

    def gather(t, then=None):
        for a in range(3):
            hi, lo = split_bf16(mom[t, a].T)
            mom_t[a * size_z : (a + 1) * size_z, 0:planes] = hi
            mom_t[a * size_z : (a + 1) * size_z, planes : 2 * planes] = lo

        def turn(n):
            return n if then is None else lax.rem(n + first_tile, tiles)

        find(turn(0), found_a)

        def two(n, _):
            first, second, third = turn(2 * n), turn(2 * n + 1), turn(lax.rem(2 * n + 2, tiles))
            find(second, found_b)
            pick(first, found_a)
            if then is not None:
                then(first)
            find(third, found_a)
            pick(second, found_b)
            if then is not None:
                then(second)
            return 0

        lax.fori_loop(0, tiles // 2, two, 0)
        if then is None:
            for a in range(3):
                slots[1 + a] = slots[1 + a] + slots[0] * (seen[a] - slots[1 + a])

    def deliver(n):
        s = pl.ds(pl.multiple_of(n * tile_rows, tile_rows), tile_rows)
        upper = pl.ds(pl.multiple_of(half_dev + n * tile_rows, tile_rows), tile_rows)
        low = lax.broadcasted_iota(i32, (tile_rows, 128), 1) < 64
        c = slots[0, s, :]
        vx, vy, vz = [
            slots[1 + a, s, :] + c * (seen[a, s, :] - slots[1 + a, s, :]) for a in range(3)
        ]
        send2[0, s, :] = jnp.where(low, vx, pltpu.roll(vy, 64, 1))
        send2[0, upper, :] = jnp.where(low, pltpu.roll(vx, 64, 1), vy)
        send2[1, s, :] = jnp.where(low, vz, 0.0)
        send2[1, upper, :] = jnp.where(low, pltpu.roll(vz, 64, 1), 0.0)
        for r in range(tile_rows):
            for side in range(2):
                o = side * half_dev + n * tile_rows + r

                @pl.when(o != me)
                def _():
                    exchange_send(send2, recv2, 1, o)

    def nb(dc, dw):
        return (lax.rem(chan + dc + n_chan, n_chan), lax.rem(width + dw + n_width, n_width))

    inner_x, inner_y = pl.ds(1, size_x), pl.ds(PAD, size_y)
    last_x, last_y = size_x, PAD + size_y - 1
    end_x, end_y = size_x + 1, PAD + size_y

    def halo_copies(t):
        g = moved.at[t % 2]
        parts_list = [
            (g.at[0:5, last_x, inner_y], g.at[0:5, 0, inner_y], nb(1, 0)),
            (g.at[8:13, 1, inner_y], g.at[8:13, end_x, inner_y], nb(-1, 0)),
            (g.at[4:9, inner_x, last_y], g.at[4:9, inner_x, PAD - 1], nb(0, 1)),
            (g.at[12:16, inner_x, PAD], g.at[12:16, inner_x, end_y], nb(0, -1)),
            (g.at[0:1, inner_x, PAD], g.at[0:1, inner_x, end_y], nb(0, -1)),
            (g.at[4, last_x, pl.ds(last_y, 1)], g.at[4, 0, pl.ds(PAD - 1, 1)], nb(1, 1)),
            (g.at[12, 1, pl.ds(PAD, 1)], g.at[12, end_x, pl.ds(end_y, 1)], nb(-1, -1)),
            (g.at[0, last_x, pl.ds(PAD, 1)], g.at[0, 0, pl.ds(end_y, 1)], nb(1, -1)),
            (g.at[8, 1, pl.ds(last_y, 1)], g.at[8, end_x, pl.ds(PAD - 1, 1)], nb(-1, 1)),
        ]
        return [
            pltpu.make_async_remote_copy(
                src, dst, halo_send.at[t, n], halo_recv.at[t, n], device_id=to, device_id_type=MESH
            )
            for n, (src, dst, to) in enumerate(parts_list)
        ]

    def load(t, i, h):
        f = []
        for k in range(19):
            if t == 0:
                f.append(pop[k, i, 8 * h : 8 * h + 8, :])
            elif k in STAY:
                f.append(stayed[(t - 1) % 2, STAY[k], i, 8 * h : 8 * h + 8, :])
            else:
                step_x, step_y, _ = LATTICE[k]
                start = PAD + 8 * h - step_y
                f.append(moved[(t - 1) % 2, SLOT_OF[k], i + 1 - step_x, start : start + 8, :])
        return f

    def step_plane(t):
        def one(i):
            coef = [coef_ref[n] for n in range(51)]
            even_c = [coef[6 * a : 6 * a + 6] for a in range(6)]
            odd_c = [
                [coef[36 + 4 * a : 38 + 4 * a], coef[38 + 4 * a : 40 + 4 * a]] for a in range(3)
            ]
            coefs = (even_c, odd_c, coef[48:51])
            for h in range(size_y // 8):
                f = load(t, i, h)
                at = pl.ds(pl.multiple_of(i * size_y + 8 * h, 8), 8)
                count = fields[0, at, :]
                held = [fields[1 + 3 * (t % 2) + a, at, :] for a in range(3)]
                memory = [fields[7 + t - 1 - s, at, :] for s in range(t)]
                seen_m = [[mom[s, a, at, :] for a in range(3)] for s in range(t)]
                solid = solid_ref[i, 8 * h : 8 * h + 8, :] == 1
                out, m = relax_group(f, (count, held, memory), seen_m, solid, coefs)
                for a in range(3):
                    mom[t, a, at, :] = m[a]
                for k in range(19):
                    value = out[k]
                    if LATTICE[k][2]:
                        value = pltpu.roll(value, LATTICE[k][2] % size_z, 1)
                    if k in STAY:
                        stayed[t % 2, STAY[k], i, 8 * h : 8 * h + 8, :] = value
                    else:
                        moved[t % 2, SLOT_OF[k], i + 1, PAD + 8 * h : PAD + 8 * h + 8, :] = value

        return one

    scatter([1, 2, 3, 0])
    coup = slots[0]
    keep = 1.0 - coup
    weights[3] = coup * coup
    pop_copy.wait()
    for t in range(STEPS):
        plane = step_plane(t)
        if t < STEPS - 1:
            for a in range(3):
                weights[a] = weights[a] * keep
            if t > 0:
                weights[3] = weights[3] * keep
            odd = (t + 1) % 2
            scatter([1 + 3 * odd, 2 + 3 * odd, 3 + 3 * odd, 7 + t], plane)
        else:

            def one(i, _):
                plane(i)
                return 0

            lax.fori_loop(0, size_x, one, 0)
        copies = halo_copies(t)
        for copy in copies:
            copy.start()
        if t < STEPS - 1:
            gather(t)
        else:
            gather(t, deliver)
        for copy in copies:
            copy.wait()

    def finish(i, _):
        for h in range(size_y // 8):
            f = load(STEPS, i, h)
            for k in range(19):
                pop[k, i, 8 * h : 8 * h + 8, :] = f[k]
        return 0

    lax.fori_loop(0, size_x, finish, 0)
    out_copy = pltpu.make_async_copy(pop, out_hbm, out_sem)
    out_copy.start()
    recv2[:, pl.ds(me, 1), :] = send2[:, pl.ds(me, 1), :]
    exchange_wait(send2, recv2, 1)

    back_out[...] = recv2[...]
    out_copy.wait()


def finish_kernel(dims, pop_hbm, back_ref, dest_ref, rank_ref, out_hbm, vel_out, held, sems):
    n_dev, parts = dims
    f32, bf16, i32 = jnp.float32, jnp.bfloat16, jnp.int32
    copies_in = [pltpu.make_async_copy(pop_hbm.at[k], held.at[k], sems.at[0, k]) for k in range(19)]
    copies_out = [
        pltpu.make_async_copy(held.at[k], out_hbm.at[k], sems.at[1, k]) for k in range(19)
    ]
    for copy in copies_in:
        copy.start()
    block = min(1024, parts)
    dev_iota = lax.broadcasted_iota(i32, (n_dev, block), 0)
    cap_iota = lax.broadcasted_iota(i32, (CAP, block), 0).astype(f32)
    back = [split_bf16(back_ref[a].T) for a in range(2)]
    back = jnp.concatenate([back[0][0], back[1][0][0:64], back[0][1], back[1][1][0:64]], axis=0)

    def unpack(b, _):
        s = pl.ds(pl.multiple_of(b * block, block), block)
        hits = jnp.where(dev_iota == dest_ref[:, s], 1.0, 0.0).astype(bf16)
        found = dot_nn(back, hits)
        hit = cap_iota == rank_ref[:, s]
        for a in range(3):
            value = found[64 * a : 64 * a + 64] + found[64 * (a + 3) : 64 * (a + 3) + 64]
            vel_out[a : a + 1, s] = jnp.sum(jnp.where(hit, value, 0.0), axis=0, keepdims=True)
        return 0

    blocks = parts // block
    lax.fori_loop(0, blocks // 4, unpack, 0)
    for arrived, leaving in zip(copies_in, copies_out):
        arrived.wait()
        leaving.start()
    lax.fori_loop(blocks // 4, blocks, unpack, 0)
    for copy in copies_out:
        copy.wait()


def per_device(
    n_chan,
    n_width,
    populations,
    moment_rates,
    solid_flags,
    destination,
    local_cell,
    particle_velocity,
    coupling,
):
    _, size_x, size_y, size_z = populations.shape
    parts = destination.shape[0]
    n_dev = n_chan * n_width
    rows = n_dev * CAP // 128
    planes = size_x * size_y
    f32, bf16 = jnp.float32, jnp.bfloat16
    vmem = pl.BlockSpec(memory_space=pltpu.VMEM)
    chunk = min(2048, rows * 128 // 2)
    tile = min(1024, rows * 128 // 2)
    destination = destination.reshape(1, parts)
    moved, back, ranks = pl.pallas_call(
        functools.partial(kernel, (n_chan, n_width, size_x, size_y, size_z, parts)),
        out_shape=(
            jax.ShapeDtypeStruct(populations.shape, f32),
            jax.ShapeDtypeStruct((2, n_dev, 128), f32),
            jax.ShapeDtypeStruct((1, parts), f32),
        ),
        in_specs=[
            pl.BlockSpec(memory_space=pl.ANY),
            pl.BlockSpec(memory_space=pltpu.SMEM),
            vmem,
            vmem,
            vmem,
            vmem,
            vmem,
        ],
        out_specs=(pl.BlockSpec(memory_space=pl.ANY), vmem, vmem),
        scratch_shapes=[
            pltpu.VMEM(populations.shape, f32),
            pltpu.VMEM((2, 16, size_x + 2, size_y + 2 * PAD, size_z), f32),
            pltpu.VMEM((2, 3, size_x, size_y, size_z), f32),
            pltpu.VMEM((n_dev, parts), bf16),
            pltpu.VMEM((10 * CAP, parts), bf16),
            pltpu.VMEM((3, n_dev, 128), f32),
            pltpu.VMEM((3, n_dev, 128), f32),
            pltpu.VMEM((2, n_dev, 128), f32),
            pltpu.VMEM((2, n_dev, 128), f32),
            pltpu.VMEM((4, rows, 128), f32),
            pltpu.VMEM((2, rows, 128), f32),
            pltpu.VMEM((4, rows, 128), f32),
            pltpu.VMEM((3, rows, 128), f32),
            pltpu.VMEM((2 * planes, rows * 128), bf16),
            pltpu.VMEM((size_z, rows * 128), bf16),
            pltpu.VMEM((8 * size_z, chunk), bf16),
            pltpu.VMEM((8 * size_z, chunk), bf16),
            pltpu.VMEM((8 * size_z, planes), f32),
            pltpu.VMEM((3 * size_z, tile), f32),
            pltpu.VMEM((3 * size_z, tile), f32),
            pltpu.VMEM((10, planes, size_z), f32),
            pltpu.VMEM((STEPS, 3, planes, size_z), f32),
            pltpu.VMEM((3 * size_z, 2 * planes), bf16),
            pltpu.VMEM((51, 8, 128), f32),
            pltpu.SemaphoreType.DMA,
            pltpu.SemaphoreType.DMA,
            pltpu.SemaphoreType.DMA((2,)),
            pltpu.SemaphoreType.DMA((2,)),
            pltpu.SemaphoreType.DMA((STEPS, 9)),
            pltpu.SemaphoreType.DMA((STEPS, 9)),
        ],
        compiler_params=pltpu.CompilerParams(
            collective_id=0, has_side_effects=True, vmem_limit_bytes=56 * 1024 * 1024
        ),
        name="lattice_steps",
    )(
        populations,
        moment_rates,
        solid_flags,
        destination,
        local_cell.reshape(1, parts),
        particle_velocity,
        coupling.reshape(1, parts),
    )
    return pl.pallas_call(
        functools.partial(finish_kernel, (n_dev, parts)),
        out_shape=(
            jax.ShapeDtypeStruct(populations.shape, f32),
            jax.ShapeDtypeStruct(particle_velocity.shape, f32),
        ),
        in_specs=[pl.BlockSpec(memory_space=pl.ANY), vmem, vmem, vmem],
        out_specs=(pl.BlockSpec(memory_space=pl.ANY), vmem),
        scratch_shapes=[
            pltpu.VMEM(populations.shape, f32),
            pltpu.SemaphoreType.DMA((2, 19)),
        ],
        compiler_params=pltpu.CompilerParams(vmem_limit_bytes=56 * 1024 * 1024),
        name="particles_back",
    )(moved, back, destination, ranks)


def solution(mesh):
    return jax.shard_map(
        functools.partial(per_device, mesh.shape["chan"], mesh.shape["width"]),
        mesh=mesh,
        in_specs=(
            P(None, "chan", "width", None),
            P(),
            P("chan", "width", None),
            P(("chan", "width"), None),
            P(("chan", "width")),
            P(None, ("chan", "width")),
            P(("chan", "width")),
        ),
        out_specs=(P(None, "chan", "width", None), P(None, ("chan", "width"))),
        check_vma=False,
    )
```

```python
import functools
import math

import jax
import jax.numpy as jnp
import numpy as np
from jax import lax
from jax.experimental import pallas as pl
from jax.experimental.pallas import tpu as pltpu
from jax.sharding import PartitionSpec as P

MESH = pl.DeviceIdType.MESH
STEPS = 4
CAP = 64
LATTICE = [
    [0, 0, 0],
    [1, 0, 0],
    [-1, 0, 0],
    [0, 1, 0],
    [0, -1, 0],
    [0, 0, 1],
    [0, 0, -1],
    [1, 1, 0],
    [-1, -1, 0],
    [1, -1, 0],
    [-1, 1, 0],
    [1, 0, 1],
    [-1, 0, -1],
    [1, 0, -1],
    [-1, 0, 1],
    [0, 1, 1],
    [0, -1, -1],
    [0, 1, -1],
    [0, -1, 1],
]
OPPOSITE = [0, 2, 1, 4, 3, 6, 5, 8, 7, 10, 9, 12, 11, 14, 13, 16, 15, 18, 17]
COUPLING_MASS = 0.02
RING = [9, 1, 11, 13, 7, 3, 15, 17, 10, 2, 12, 14, 8, 4, 16, 18]
SLOT_OF = {k: i for i, k in enumerate(RING)}
STAY = {0: 0, 5: 1, 6: 2}
PAD = 8
DIAGONALS = [(0, 1, 7), (0, 2, 11), (1, 2, 15)]


def moment_basis():
    lattice_np = np.array(LATTICE, dtype=np.float32)
    along_x, along_y, along_z = (lattice_np[:, 0], lattice_np[:, 1], lattice_np[:, 2])
    columns = [
        np.ones(19, dtype=np.float32),
        along_x,
        along_y,
        along_z,
        along_x * along_x,
        along_y * along_y,
        along_z * along_z,
        along_x * along_y,
        along_x * along_z,
        along_y * along_z,
        along_x * along_y * along_y,
        along_x * along_z * along_z,
        along_y * along_x * along_x,
        along_y * along_z * along_z,
        along_z * along_x * along_x,
        along_z * along_y * along_y,
        along_x * along_x * along_y * along_y,
        along_x * along_x * along_z * along_z,
        along_y * along_y * along_z * along_z,
    ]
    found_cols = []
    for column in columns:
        vector = np.array(column, dtype=np.float32)
        for repeat_pass in range(2):
            for earlier in found_cols:
                vector = vector - float(np.dot(earlier, vector)) * earlier
        found_cols.append((vector / math.sqrt(float(np.dot(vector, vector)))).astype(np.float32))
    return np.stack(found_cols[4:], axis=1).astype(np.float32)


def sector_tables():
    basis = moment_basis().astype(np.float64)

    def vec(entries):
        v = np.zeros(19)
        for k, s in entries:
            v[k] = s
        return v

    def project(members):
        m = np.stack(members)
        dots = m @ basis
        dots[np.abs(dots) < 1e-5] = 0.0
        sizes = np.sum(np.abs(m), axis=1)
        return dots[:, None, :] * dots[None, :, :] / sizes[None, :, None]

    even = [vec([(0, 1)])]
    for a in range(3):
        even.append(vec([(1 + 2 * a, 1), (2 + 2 * a, 1)]))
    for a, b, k in DIAGONALS:
        even.append(vec([(k + i, 1) for i in range(4)]))
    table = project(even)
    table = table[1:, 1:] - table[1:, :1]
    table[:3] *= 0.5
    table[3:] *= 0.25
    even_table = table
    odd_tables = []
    for a in range(3):
        members = [vec([(1 + 2 * a, 1), (2 + 2 * a, -1)])]
        for p, q, k in DIAGONALS:
            if a in (p, q):
                members.append(vec([(k + i, LATTICE[k + i][a]) for i in range(4)]))
        table = project(members)
        odd_tables.append((table[1:, 1:] - table[1:, :1]) * 0.25)
    cross = []
    for p, q, k in DIAGONALS:
        table = project([vec([(k + i, LATTICE[k + i][p] * LATTICE[k + i][q]) for i in range(4)])])
        cross.append(table[0, 0] * 0.25)
    return even_table, odd_tables, cross


def weigh(rates, weights):
    total = None
    for j in range(15):
        if abs(weights[j]) > 1e-9:
            term = rates[j] * float(weights[j])
            total = term if total is None else total + term
    return total if total is not None else jnp.zeros_like(rates[0])


def split_bf16(x):
    hi = x.astype(jnp.bfloat16)
    lo = (x - hi.astype(jnp.float32)).astype(jnp.bfloat16)
    return hi, lo


def dot_nt(a, b):
    return lax.dot_general(a, b, (((1,), (1,)), ((), ())), preferred_element_type=jnp.float32)


def dot_nn(a, b):
    return lax.dot_general(a, b, (((1,), (0,)), ((), ())), preferred_element_type=jnp.float32)


def relax_group(f, fields, seen_m, solid, coef):
    even_c, odd_c, cross_c = coef
    sums, diffs = [], []
    for a in range(3):
        p, n = f[1 + 2 * a], f[2 + 2 * a]
        sums.append(p + n)
        diffs.append(p - n)
    diag_sum, diag_cross, diag_first, diag_second = [], [], [], []
    for p, q, k in DIAGONALS:
        a1, b1 = f[k] + f[k + 1], f[k] - f[k + 1]
        a2, b2 = f[k + 2] + f[k + 3], f[k + 2] - f[k + 3]
        diag_sum.append(a1 + a2)
        diag_cross.append(a1 - a2)
        diag_first.append(b1 + b2)
        diag_second.append(b1 - b2)
    odd = [[], [], []]
    for g, (p, q, k) in enumerate(DIAGONALS):
        odd[p].append(diag_first[g])
        odd[q].append(diag_second[g])
    mom = [diffs[a] + (odd[a][0] + odd[a][1]) for a in range(3)]
    density = f[0] + ((sums[0] + sums[1]) + sums[2]) + ((diag_sum[0] + diag_sum[1]) + diag_sum[2])
    count, held, memory = fields
    force = []
    for a in range(3):
        kept = held[a]
        for weight, earlier in zip(memory, seen_m):
            kept = kept + weight * earlier[a]
        force.append(COUPLING_MASS * (kept - count * mom[a]))
    half = [0.5 * force[a] for a in range(3)]
    vel = [mom[a] + half[a] for a in range(3)]
    press = [mom[a] * mom[a] - half[a] * half[a] for a in range(3)]
    press_sum = press[0] + press[1] + press[2]
    work = [vel[a] * force[a] for a in range(3)]
    work_third = (work[0] + work[1] + work[2]) * (1.0 / 3.0)
    base = density * (1.0 / 9.0) - press_sum * (1.0 / 6.0)
    gaps = []
    for a in range(3):
        gaps.append(base + 0.5 * press[a] - sums[a])
    for g, (p, q, k) in enumerate(DIAGONALS):
        gaps.append(base + 0.5 * (press[p] + press[q]) - diag_sum[g])
    change = []
    for a in range(6):
        total = even_c[a][0] * gaps[0]
        for b in range(1, 6):
            total = total + even_c[a][b] * gaps[b]
        if a < 3:
            total = total + 0.5 * (work[a] - work_third)
        else:
            p, q, k = DIAGONALS[a - 3]
            total = total + 0.25 * (work[p] + work[q] - work_third)
        change.append(total)
    rest = f[0] - 2.0 * (change[0] + change[1] + change[2]) - 4.0 * (change[3] + change[4] + change[5])
    odd_axis, odd_diag = [], []
    for a in range(3):
        third = mom[a] * (1.0 / 3.0)
        g1, g2 = third - odd[a][0], third - odd[a][1]
        d1 = odd_c[a][0][0] * g1 + odd_c[a][0][1] * g2
        d2 = odd_c[a][1][0] * g1 + odd_c[a][1][1] * g2
        push = force[a] * (1.0 / 12.0)
        odd_axis.append(2.0 * (push - (d1 + d2)))
        odd_diag.append([push + d1, push + d2])
    out = [None] * 19
    out[0] = rest
    for a in range(3):
        out[1 + 2 * a] = f[1 + 2 * a] + (change[a] + odd_axis[a])
        out[2 + 2 * a] = f[2 + 2 * a] + (change[a] - odd_axis[a])
    place = [0, 0, 0]
    for g, (p, q, k) in enumerate(DIAGONALS):
        o1, o2 = odd_diag[p][place[p]], odd_diag[q][place[q]]
        place[p] += 1
        place[q] += 1
        gap = mom[p] * mom[q] - half[p] * half[q] - diag_cross[g]
        cross = cross_c[g] * gap + 0.25 * (vel[p] * force[q] + vel[q] * force[p])
        s_plus, s_minus = change[3 + g] + cross, change[3 + g] - cross
        o_plus, o_minus = o1 + o2, o1 - o2
        out[k] = f[k] + (s_plus + o_plus)
        out[k + 1] = f[k + 1] + (s_plus - o_plus)
        out[k + 2] = f[k + 2] + (s_minus + o_minus)
        out[k + 3] = f[k + 3] + (s_minus - o_minus)
    out = [jnp.where(solid, f[OPPOSITE[k]], out[k]) for k in range(19)]
    return out, mom


def kernel(
    dims,
    pop_hbm,
    rates_ref,
    solid_ref,
    dest_ref,
    cell_ref,
    vel_ref,
    coup_ref,
    out_hbm,
    back_out,
    rank_rows,
    pop,
    moved,
    stayed,
    own_hits,
    packing,
    send1,
    recv1,
    send2,
    recv2,
    slots,
    cells,
    weights,
    seen,
    plane_hits,
    slot_hits,
    depth_hits,
    spread_a,
    spread_b,
    summed,
    found_a,
    found_b,
    fields,
    mom,
    mom_t,
    coef_ref,
    pop_sem,
    out_sem,
    a2a_send,
    a2a_recv,
    halo_send,
    halo_recv,
):
    n_chan, n_width, size_x, size_y, size_z, parts = dims
    n_dev = n_chan * n_width
    rows = n_dev * CAP // 128
    planes = size_x * size_y
    chan, width = lax.axis_index("chan"), lax.axis_index("width")
    me = chan * n_width + width
    f32, bf16, i32 = jnp.float32, jnp.bfloat16, jnp.int32

    barrier = pltpu.get_barrier_semaphore()

    def wrap(x, n):
        return jnp.where(x >= n, x - n, x)

    across = [n_width // 2 + (1 - 2 * (j % 2)) * ((j + 1) // 2) for j in range(n_width - 1)] + [0]
    widths = [wrap(width + d, n_width) for d in across]

    def each_peer(act):
        def one(j, _):
            odd = lax.rem(j, 2)
            d = n_chan // 2 + (1 - 2 * odd) * ((j + odd) // 2)
            c = wrap(chan + d, n_chan)
            for w in widths:
                act(c, w)
            return 0

        lax.fori_loop(0, n_chan - 1, one, 0, unroll=3)
        for w in widths[:-1]:
            act(chan, w)

    def greet(c, w):
        pl.semaphore_signal(barrier, inc=1, device_id=(c, w), device_id_type=MESH)

    each_peer(greet)
    pop_copy = pltpu.make_async_copy(pop_hbm, pop, pop_sem)
    pop_copy.start()

    even_table, odd_tables, cross_table = sector_tables()
    rates = [jnp.full((8, 128), rates_ref[j], f32) for j in range(15)]
    places = 0
    for a in range(6):
        for b in range(6):
            coef_ref[places] = weigh(rates, even_table[a, b])
            places += 1
    for axis in range(3):
        for a in range(2):
            for b in range(2):
                coef_ref[places] = weigh(rates, odd_tables[axis][a, b])
                places += 1
    for g in range(3):
        coef_ref[places] = weigh(rates, cross_table[g])
        places += 1

    block = 256
    tri = (
        lax.broadcasted_iota(i32, (block, block), 0) <= lax.broadcasted_iota(i32, (block, block), 1)
    ).astype(f32).astype(bf16)
    dev_iota = lax.broadcasted_iota(i32, (n_dev, block), 0)
    cap_iota = lax.broadcasted_iota(i32, (CAP, block), 0).astype(f32)

    def pack(b, before):
        s = pl.ds(pl.multiple_of(b * block, block), block)
        hits = jnp.where(dev_iota == dest_ref[:, s], 1.0, 0.0)
        hits_b = hits.astype(bf16)
        own_hits[:, s] = hits_b
        upto = dot_nn(hits_b, tri)
        rank = jnp.sum(hits * (upto + before), axis=0, keepdims=True) - 1.0
        rank_rows[:, s] = rank
        rank_hit = cap_iota == rank
        cell = cell_ref[:, s]
        pieces = []
        for value in (coup_ref[:, s], vel_ref[0:1, s], vel_ref[1:2, s], vel_ref[2:3, s]):
            pieces.append(split_bf16(value))
        order = [pieces[0][0], pieces[1][0], pieces[0][1], pieces[1][1]]
        order += [pieces[2][0], pieces[3][0], pieces[2][1], pieces[3][1]]
        order = [piece.astype(f32) for piece in order]
        order += [(cell // 128).astype(f32), lax.rem(cell, 128).astype(f32)]
        for j, row in enumerate(order):
            packing[j * CAP : (j + 1) * CAP, s] = jnp.where(rank_hit, row, 0.0).astype(bf16)
        return before + upto[:, block - 1 : block]

    lax.fori_loop(0, parts // block, pack, jnp.zeros((n_dev, 1), f32), unroll=4)
    packed = dot_nt(own_hits[...], packing[...])
    low = lax.broadcasted_iota(i32, (n_dev, 128), 1) < 64
    send1[0] = packed[:, 0:128] + packed[:, 128:256]
    send1[1] = packed[:, 256:384] + packed[:, 384:512]
    last = packed[:, 512:640]
    send1[2] = jnp.where(low, last * 128.0 + pltpu.roll(last, 64, 1), 0.0)

    pl.semaphore_wait(barrier, n_dev - 1)

    def exchange_send(src, dst, which, c, w):
        o = c * n_width + w
        pltpu.make_async_remote_copy(
            src.at[:, pl.ds(o, 1)],
            dst.at[:, pl.ds(me, 1)],
            a2a_send.at[which],
            a2a_recv.at[which],
            device_id=(c, w),
            device_id_type=MESH,
        ).start()

    def exchange_wait(src, dst, which):
        part = pl.ds(0, n_dev - 1)
        pltpu.make_async_copy(dst.at[:, part], dst.at[:, part], a2a_recv.at[which]).wait()
        pltpu.make_async_copy(src.at[:, part], src.at[:, part], a2a_send.at[which]).wait()

    each_peer(functools.partial(exchange_send, send1, recv1, 0))
    recv1[:, pl.ds(me, 1), :] = send1[:, pl.ds(me, 1), :]
    exchange_wait(send1, recv1, 0)

    half_dev = n_dev // 2
    low = lax.broadcasted_iota(i32, (half_dev, 128), 1) < 64

    def both(ref):
        first, second = ref[0:half_dev, :], ref[half_dev:n_dev, :]
        return (
            jnp.where(low, first, pltpu.roll(second, 64, 1)),
            jnp.where(low, pltpu.roll(first, 64, 1), second),
        )

    coup, vx = both(recv1[0])
    vy, vz = both(recv1[1])
    cell = both(recv1[2])[0].astype(i32)
    slots[0], slots[1], slots[2], slots[3] = coup, vx, vy, vz
    cells[0] = (cell // 128).astype(f32)
    cells[1] = lax.rem(cell, 128).astype(f32)
    weights[0], weights[1], weights[2] = coup * vx, coup * vy, coup * vz
    weights[3] = coup

    plane_iota = lax.broadcasted_iota(i32, (planes, 128), 0).astype(f32)
    plane_lanes = lax.broadcasted_iota(i32, (128, planes), 1).astype(f32)
    depth_iota = lax.broadcasted_iota(i32, (size_z, 128), 0).astype(f32)

    def place(n, _):
        columns = cells[0, pl.ds(pl.multiple_of(8 * n, 8), 8), :].T
        for r in range(8):
            i = 8 * n + r
            s = pl.ds(pl.multiple_of(i * 128, 128), 128)
            hits = jnp.where(plane_iota == cells[0, pl.ds(i, 1), :], 1.0, 0.0).astype(bf16)
            plane_hits[0:planes, s] = hits
            plane_hits[planes : 2 * planes, s] = hits
            hits = jnp.where(depth_iota == cells[1, pl.ds(i, 1), :], 1.0, 0.0)
            depth_hits[:, s] = hits.astype(bf16)
            hits = jnp.where(plane_lanes == columns[:, r : r + 1], 1.0, 0.0)
            slot_hits[s, :] = hits.astype(bf16)
        return 0

    lax.fori_loop(0, rows // 8, place, 0)

    chunk = min(2048, rows * 128 // 2)
    chunk_rows = chunk // 128

    chunks = rows // chunk_rows

    def weigh_chunk(n, spread):
        for r in range(chunk_rows):
            i = n * chunk_rows + r
            hits = depth_hits[:, pl.ds(pl.multiple_of(i * 128, 128), 128)]
            hits = hits.reshape(size_z // 16, 16, 128)
            for j in range(4):
                value = jnp.broadcast_to(weights[j, pl.ds(i, 1), :], (16, 128))
                for h, piece in enumerate(split_bf16(value)):
                    at = (2 * j + h) * size_z
                    spread[at : at + size_z, r * 128 : (r + 1) * 128] = (
                        hits * piece[None]
                    ).reshape(size_z, 128)

    def add_chunk(n, spread):
        s = pl.ds(pl.multiple_of(n * chunk, chunk), chunk)
        summed[...] += dot_nn(spread[...], slot_hits[s, :])

    def ends_first(i):
        return jnp.where(i == 0, 0, jnp.where(i == 1, size_x - 1, i - 1))

    def scatter(targets, beside=None, early=None):
        summed[...] = jnp.zeros_like(summed)
        share = size_x // chunks

        def two(n, _):
            for part, spread in enumerate((spread_a, spread_b)):
                weigh_chunk(2 * n + part, spread)
                add_chunk(2 * n + part, spread)
                if beside is not None:
                    for i in range(share):
                        beside(ends_first((2 * n + part) * share + i))
            if early is not None:

                @pl.when(n == 0)
                def _():
                    early()

            return 0

        lax.fori_loop(0, chunks // 2, two, 0)
        for j, target in enumerate(targets):
            at = 2 * j * size_z
            total = summed[at : at + size_z, :] + summed[at + size_z : at + 2 * size_z, :]
            fields[target] = total.T

    tile = min(1024, rows * 128 // 2)
    tile_rows = tile // 128

    def find(n, found):
        s = pl.ds(pl.multiple_of(n * tile, tile), tile)
        found[...] = dot_nn(mom_t[...], plane_hits[:, s])

    def pick(n, found):
        for r in range(tile_rows):
            i = n * tile_rows + r
            hit = depth_iota == cells[1, pl.ds(i, 1), :]
            for a in range(3):
                both = found[a * size_z : (a + 1) * size_z, r * 128 : (r + 1) * 128]
                seen[a, pl.ds(i, 1), :] = jnp.sum(
                    jnp.where(hit, both, 0.0), axis=0, keepdims=True
                )

    tiles = rows // tile_rows
    first_tile = lax.rem(me, rows) // tile_rows

    def gather(t, then=None):
        for a in range(3):
            hi, lo = split_bf16(mom[t, a].T)
            mom_t[a * size_z : (a + 1) * size_z, 0:planes] = hi
            mom_t[a * size_z : (a + 1) * size_z, planes : 2 * planes] = lo

        def turn(n):
            return n if then is None else lax.rem(n + first_tile, tiles)

        find(turn(0), found_a)

        def two(n, _):
            first, second, third = turn(2 * n), turn(2 * n + 1), turn(lax.rem(2 * n + 2, tiles))
            find(second, found_b)
            pick(first, found_a)
            if then is not None:
                then(first)
            find(third, found_a)
            pick(second, found_b)
            if then is not None:
                then(second)
            return 0

        lax.fori_loop(0, tiles // 2, two, 0)
        if then is None:
            for a in range(3):
                slots[1 + a] = slots[1 + a] + slots[0] * (seen[a] - slots[1 + a])

    def deliver(n):
        s = pl.ds(pl.multiple_of(n * tile_rows, tile_rows), tile_rows)
        upper = pl.ds(pl.multiple_of(half_dev + n * tile_rows, tile_rows), tile_rows)
        low = lax.broadcasted_iota(i32, (tile_rows, 128), 1) < 64
        c = slots[0, s, :]
        vx, vy, vz = [
            slots[1 + a, s, :] + c * (seen[a, s, :] - slots[1 + a, s, :]) for a in range(3)
        ]
        send2[0, s, :] = jnp.where(low, vx, pltpu.roll(vy, 64, 1))
        send2[0, upper, :] = jnp.where(low, pltpu.roll(vx, 64, 1), vy)
        send2[1, s, :] = jnp.where(low, vz, 0.0)
        send2[1, upper, :] = jnp.where(low, pltpu.roll(vz, 64, 1), 0.0)
        for r in range(tile_rows):
            for side in range(2):
                c = (side * half_dev + r) // n_width + n * (tile_rows // n_width)
                w = r % n_width

                @pl.when(jnp.logical_or(c != chan, w != width))
                def _():
                    exchange_send(send2, recv2, 1, c, w)

    def nb(dc, dw):
        return (lax.rem(chan + dc + n_chan, n_chan), lax.rem(width + dw + n_width, n_width))

    inner_x, inner_y = pl.ds(1, size_x), pl.ds(PAD, size_y)
    last_x, last_y = size_x, PAD + size_y - 1
    end_x, end_y = size_x + 1, PAD + size_y

    def halo_copy(t, n):
        g = moved.at[t % 2]
        parts_list = [
            (g.at[0:5, last_x, inner_y], g.at[0:5, 0, inner_y], nb(1, 0)),
            (g.at[8:13, 1, inner_y], g.at[8:13, end_x, inner_y], nb(-1, 0)),
            (g.at[4:9, inner_x, last_y], g.at[4:9, inner_x, PAD - 1], nb(0, 1)),
            (g.at[12:16, inner_x, PAD], g.at[12:16, inner_x, end_y], nb(0, -1)),
            (g.at[0:1, inner_x, PAD], g.at[0:1, inner_x, end_y], nb(0, -1)),
            (g.at[4, last_x, pl.ds(last_y, 1)], g.at[4, 0, pl.ds(PAD - 1, 1)], nb(1, 1)),
            (g.at[12, 1, pl.ds(PAD, 1)], g.at[12, end_x, pl.ds(end_y, 1)], nb(-1, -1)),
            (g.at[0, last_x, pl.ds(PAD, 1)], g.at[0, 0, pl.ds(end_y, 1)], nb(1, -1)),
            (g.at[8, 1, pl.ds(last_y, 1)], g.at[8, end_x, pl.ds(PAD - 1, 1)], nb(-1, 1)),
        ]
        src, dst, to = parts_list[n]
        return pltpu.make_async_remote_copy(
            src, dst, halo_send.at[t, n], halo_recv.at[t, n], device_id=to, device_id_type=MESH
        )

    def load(t, i, h):
        f = []
        for k in range(19):
            if t == 0:
                f.append(pop[k, i, 8 * h : 8 * h + 8, :])
            elif k in STAY:
                f.append(stayed[(t - 1) % 2, STAY[k], i, 8 * h : 8 * h + 8, :])
            else:
                step_x, step_y, _ = LATTICE[k]
                start = PAD + 8 * h - step_y
                f.append(moved[(t - 1) % 2, SLOT_OF[k], i + 1 - step_x, start : start + 8, :])
        return f

    def step_plane(t):
        def one(i):
            coef = [coef_ref[n] for n in range(51)]
            even_c = [coef[6 * a : 6 * a + 6] for a in range(6)]
            odd_c = [
                [coef[36 + 4 * a : 38 + 4 * a], coef[38 + 4 * a : 40 + 4 * a]] for a in range(3)
            ]
            coefs = (even_c, odd_c, coef[48:51])
            for h in range(size_y // 8):
                f = load(t, i, h)
                at = pl.ds(pl.multiple_of(i * size_y + 8 * h, 8), 8)
                count = fields[0, at, :]
                held = [fields[1 + 3 * (t % 2) + a, at, :] for a in range(3)]
                memory = [fields[7 + t - 1 - s, at, :] for s in range(t)]
                seen_m = [[mom[s, a, at, :] for a in range(3)] for s in range(t)]
                solid = solid_ref[i, 8 * h : 8 * h + 8, :] == 1
                out, m = relax_group(f, (count, held, memory), seen_m, solid, coefs)
                for a in range(3):
                    mom[t, a, at, :] = m[a]
                for k in range(19):
                    value = out[k]
                    if LATTICE[k][2]:
                        value = pltpu.roll(value, LATTICE[k][2] % size_z, 1)
                    if k in STAY:
                        stayed[t % 2, STAY[k], i, 8 * h : 8 * h + 8, :] = value
                    else:
                        moved[t % 2, SLOT_OF[k], i + 1, PAD + 8 * h : PAD + 8 * h + 8, :] = value

        return one

    scatter([1, 2, 3, 0])
    coup = slots[0]
    keep = 1.0 - coup
    weights[3] = coup * coup
    pop_copy.wait()
    for t in range(STEPS):
        plane = step_plane(t)

        def send_ends():
            for n in (5, 6, 7, 8, 0, 1):
                halo_copy(t, n).start()

        if t < STEPS - 1:
            for a in range(3):
                weights[a] = weights[a] * keep
            if t > 0:
                weights[3] = weights[3] * keep
            odd = (t + 1) % 2
            scatter([1 + 3 * odd, 2 + 3 * odd, 3 + 3 * odd, 7 + t], plane, send_ends)
        else:

            def one(i, _):
                plane(i)
                return 0

            plane(0)
            plane(size_x - 1)
            send_ends()
            lax.fori_loop(1, size_x - 1, one, 0, unroll=2)
        for n in (2, 3, 4):
            halo_copy(t, n).start()
        if t < STEPS - 1:
            gather(t)
        else:
            gather(t, deliver)
        for n in range(9):
            halo_copy(t, n).wait()

    def finish(i, _):
        for h in range(size_y // 8):
            f = load(STEPS, i, h)
            for k in range(19):
                pop[k, i, 8 * h : 8 * h + 8, :] = f[k]
        return 0

    lax.fori_loop(0, size_x, finish, 0)
    out_copy = pltpu.make_async_copy(pop, out_hbm, out_sem)
    out_copy.start()
    recv2[:, pl.ds(me, 1), :] = send2[:, pl.ds(me, 1), :]
    exchange_wait(send2, recv2, 1)

    back_out[...] = recv2[...]
    out_copy.wait()


def finish_kernel(dims, pop_hbm, back_ref, dest_ref, rank_ref, out_hbm, vel_out, held, sems):
    n_dev, parts = dims
    f32, bf16, i32 = jnp.float32, jnp.bfloat16, jnp.int32
    copies_in = [pltpu.make_async_copy(pop_hbm.at[k], held.at[k], sems.at[0, k]) for k in range(19)]
    copies_out = [
        pltpu.make_async_copy(held.at[k], out_hbm.at[k], sems.at[1, k]) for k in range(19)
    ]
    for copy in copies_in:
        copy.start()
    block = min(1024, parts)
    dev_iota = lax.broadcasted_iota(i32, (n_dev, block), 0)
    cap_iota = lax.broadcasted_iota(i32, (CAP, block), 0).astype(f32)
    back = [split_bf16(back_ref[a].T) for a in range(2)]
    back = jnp.concatenate([back[0][0], back[1][0][0:64], back[0][1], back[1][1][0:64]], axis=0)

    def unpack(b, _):
        s = pl.ds(pl.multiple_of(b * block, block), block)
        hits = jnp.where(dev_iota == dest_ref[:, s], 1.0, 0.0).astype(bf16)
        found = dot_nn(back, hits)
        hit = cap_iota == rank_ref[:, s]
        for a in range(3):
            value = found[64 * a : 64 * a + 64] + found[64 * (a + 3) : 64 * (a + 3) + 64]
            vel_out[a : a + 1, s] = jnp.sum(jnp.where(hit, value, 0.0), axis=0, keepdims=True)
        return 0

    blocks = parts // block
    lax.fori_loop(0, blocks // 4, unpack, 0)
    for arrived, leaving in zip(copies_in, copies_out):
        arrived.wait()
        leaving.start()
    lax.fori_loop(blocks // 4, blocks, unpack, 0)
    for copy in copies_out:
        copy.wait()


def per_device(
    n_chan,
    n_width,
    populations,
    moment_rates,
    solid_flags,
    destination,
    local_cell,
    particle_velocity,
    coupling,
):
    _, size_x, size_y, size_z = populations.shape
    parts = destination.shape[0]
    n_dev = n_chan * n_width
    rows = n_dev * CAP // 128
    planes = size_x * size_y
    f32, bf16 = jnp.float32, jnp.bfloat16
    vmem = pl.BlockSpec(memory_space=pltpu.VMEM)
    chunk = min(2048, rows * 128 // 2)
    tile = min(1024, rows * 128 // 2)
    destination = destination.reshape(1, parts)
    moved, back, ranks = pl.pallas_call(
        functools.partial(kernel, (n_chan, n_width, size_x, size_y, size_z, parts)),
        out_shape=(
            jax.ShapeDtypeStruct(populations.shape, f32),
            jax.ShapeDtypeStruct((2, n_dev, 128), f32),
            jax.ShapeDtypeStruct((1, parts), f32),
        ),
        in_specs=[
            pl.BlockSpec(memory_space=pl.ANY),
            pl.BlockSpec(memory_space=pltpu.SMEM),
            vmem,
            vmem,
            vmem,
            vmem,
            vmem,
        ],
        out_specs=(pl.BlockSpec(memory_space=pl.ANY), vmem, vmem),
        scratch_shapes=[
            pltpu.VMEM(populations.shape, f32),
            pltpu.VMEM((2, 16, size_x + 2, size_y + 2 * PAD, size_z), f32),
            pltpu.VMEM((2, 3, size_x, size_y, size_z), f32),
            pltpu.VMEM((n_dev, parts), bf16),
            pltpu.VMEM((10 * CAP, parts), bf16),
            pltpu.VMEM((3, n_dev, 128), f32),
            pltpu.VMEM((3, n_dev, 128), f32),
            pltpu.VMEM((2, n_dev, 128), f32),
            pltpu.VMEM((2, n_dev, 128), f32),
            pltpu.VMEM((4, rows, 128), f32),
            pltpu.VMEM((2, rows, 128), f32),
            pltpu.VMEM((4, rows, 128), f32),
            pltpu.VMEM((3, rows, 128), f32),
            pltpu.VMEM((2 * planes, rows * 128), bf16),
            pltpu.VMEM((rows * 128, planes), bf16),
            pltpu.VMEM((size_z, rows * 128), bf16),
            pltpu.VMEM((8 * size_z, chunk), bf16),
            pltpu.VMEM((8 * size_z, chunk), bf16),
            pltpu.VMEM((8 * size_z, planes), f32),
            pltpu.VMEM((3 * size_z, tile), f32),
            pltpu.VMEM((3 * size_z, tile), f32),
            pltpu.VMEM((10, planes, size_z), f32),
            pltpu.VMEM((STEPS, 3, planes, size_z), f32),
            pltpu.VMEM((3 * size_z, 2 * planes), bf16),
            pltpu.VMEM((51, 8, 128), f32),
            pltpu.SemaphoreType.DMA,
            pltpu.SemaphoreType.DMA,
            pltpu.SemaphoreType.DMA((2,)),
            pltpu.SemaphoreType.DMA((2,)),
            pltpu.SemaphoreType.DMA((STEPS, 9)),
            pltpu.SemaphoreType.DMA((STEPS, 9)),
        ],
        compiler_params=pltpu.CompilerParams(
            collective_id=0, has_side_effects=True, vmem_limit_bytes=56 * 1024 * 1024
        ),
        name="lattice_steps",
    )(
        populations,
        moment_rates,
        solid_flags,
        destination,
        local_cell.reshape(1, parts),
        particle_velocity,
        coupling.reshape(1, parts),
    )
    return pl.pallas_call(
        functools.partial(finish_kernel, (n_dev, parts)),
        out_shape=(
            jax.ShapeDtypeStruct(populations.shape, f32),
            jax.ShapeDtypeStruct(particle_velocity.shape, f32),
        ),
        in_specs=[pl.BlockSpec(memory_space=pl.ANY), vmem, vmem, vmem],
        out_specs=(pl.BlockSpec(memory_space=pl.ANY), vmem),
        scratch_shapes=[
            pltpu.VMEM(populations.shape, f32),
            pltpu.SemaphoreType.DMA((2, 19)),
        ],
        compiler_params=pltpu.CompilerParams(vmem_limit_bytes=56 * 1024 * 1024),
        name="particles_back",
    )(moved, back, destination, ranks)


def solution(mesh):
    return jax.shard_map(
        functools.partial(per_device, mesh.shape["chan"], mesh.shape["width"]),
        mesh=mesh,
        in_specs=(
            P(None, "chan", "width", None),
            P(),
            P("chan", "width", None),
            P(("chan", "width"), None),
            P(("chan", "width")),
            P(None, ("chan", "width")),
            P(("chan", "width")),
        ),
        out_specs=(P(None, "chan", "width", None), P(None, ("chan", "width"))),
        check_vma=False,
    )
```

```python
import functools
import math

import jax
import jax.numpy as jnp
import numpy as np
from jax import lax
from jax.experimental import pallas as pl
from jax.experimental.pallas import tpu as pltpu
from jax.sharding import PartitionSpec as P

MESH = pl.DeviceIdType.MESH
STEPS = 4
CAP = 64
PIECES = 4
LATTICE = [
    [0, 0, 0],
    [1, 0, 0],
    [-1, 0, 0],
    [0, 1, 0],
    [0, -1, 0],
    [0, 0, 1],
    [0, 0, -1],
    [1, 1, 0],
    [-1, -1, 0],
    [1, -1, 0],
    [-1, 1, 0],
    [1, 0, 1],
    [-1, 0, -1],
    [1, 0, -1],
    [-1, 0, 1],
    [0, 1, 1],
    [0, -1, -1],
    [0, 1, -1],
    [0, -1, 1],
]
OPPOSITE = [0, 2, 1, 4, 3, 6, 5, 8, 7, 10, 9, 12, 11, 14, 13, 16, 15, 18, 17]
COUPLING_MASS = 0.02
RING = [9, 1, 11, 13, 7, 3, 15, 17, 10, 2, 12, 14, 8, 4, 16, 18]
SLOT_OF = {k: i for i, k in enumerate(RING)}
STAY = {0: 0, 5: 1, 6: 2}
PAD = 8
DIAGONALS = [(0, 1, 7), (0, 2, 11), (1, 2, 15)]


def moment_basis():
    lattice_np = np.array(LATTICE, dtype=np.float32)
    along_x, along_y, along_z = (lattice_np[:, 0], lattice_np[:, 1], lattice_np[:, 2])
    columns = [
        np.ones(19, dtype=np.float32),
        along_x,
        along_y,
        along_z,
        along_x * along_x,
        along_y * along_y,
        along_z * along_z,
        along_x * along_y,
        along_x * along_z,
        along_y * along_z,
        along_x * along_y * along_y,
        along_x * along_z * along_z,
        along_y * along_x * along_x,
        along_y * along_z * along_z,
        along_z * along_x * along_x,
        along_z * along_y * along_y,
        along_x * along_x * along_y * along_y,
        along_x * along_x * along_z * along_z,
        along_y * along_y * along_z * along_z,
    ]
    found_cols = []
    for column in columns:
        vector = np.array(column, dtype=np.float32)
        for repeat_pass in range(2):
            for earlier in found_cols:
                vector = vector - float(np.dot(earlier, vector)) * earlier
        found_cols.append((vector / math.sqrt(float(np.dot(vector, vector)))).astype(np.float32))
    return np.stack(found_cols[4:], axis=1).astype(np.float32)


def sector_tables():
    basis = moment_basis().astype(np.float64)

    def vec(entries):
        v = np.zeros(19)
        for k, s in entries:
            v[k] = s
        return v

    def project(members):
        m = np.stack(members)
        dots = m @ basis
        dots[np.abs(dots) < 1e-5] = 0.0
        sizes = np.sum(np.abs(m), axis=1)
        return dots[:, None, :] * dots[None, :, :] / sizes[None, :, None]

    even = [vec([(0, 1)])]
    for a in range(3):
        even.append(vec([(1 + 2 * a, 1), (2 + 2 * a, 1)]))
    for a, b, k in DIAGONALS:
        even.append(vec([(k + i, 1) for i in range(4)]))
    table = project(even)
    table = table[1:, 1:] - table[1:, :1]
    table[:3] *= 0.5
    table[3:] *= 0.25
    even_table = table
    odd_tables = []
    for a in range(3):
        members = [vec([(1 + 2 * a, 1), (2 + 2 * a, -1)])]
        for p, q, k in DIAGONALS:
            if a in (p, q):
                members.append(vec([(k + i, LATTICE[k + i][a]) for i in range(4)]))
        table = project(members)
        odd_tables.append((table[1:, 1:] - table[1:, :1]) * 0.25)
    cross = []
    for p, q, k in DIAGONALS:
        table = project([vec([(k + i, LATTICE[k + i][p] * LATTICE[k + i][q]) for i in range(4)])])
        cross.append(table[0, 0] * 0.25)
    return even_table, odd_tables, cross


def weigh(rates, weights):
    total = None
    for j in range(15):
        if abs(weights[j]) > 1e-9:
            term = rates[j] * float(weights[j])
            total = term if total is None else total + term
    return total if total is not None else jnp.zeros_like(rates[0])


def split_bf16(x):
    hi = x.astype(jnp.bfloat16)
    lo = (x - hi.astype(jnp.float32)).astype(jnp.bfloat16)
    return hi, lo


def dot_nt(a, b):
    return lax.dot_general(a, b, (((1,), (1,)), ((), ())), preferred_element_type=jnp.float32)


def dot_nn(a, b):
    return lax.dot_general(a, b, (((1,), (0,)), ((), ())), preferred_element_type=jnp.float32)


def relax_group(f, fields, seen_m, solid, coef):
    even_c, odd_c, cross_c = coef
    sums, diffs = [], []
    for a in range(3):
        p, n = f[1 + 2 * a], f[2 + 2 * a]
        sums.append(p + n)
        diffs.append(p - n)
    diag_sum, diag_cross, diag_first, diag_second = [], [], [], []
    for p, q, k in DIAGONALS:
        a1, b1 = f[k] + f[k + 1], f[k] - f[k + 1]
        a2, b2 = f[k + 2] + f[k + 3], f[k + 2] - f[k + 3]
        diag_sum.append(a1 + a2)
        diag_cross.append(a1 - a2)
        diag_first.append(b1 + b2)
        diag_second.append(b1 - b2)
    odd = [[], [], []]
    for g, (p, q, k) in enumerate(DIAGONALS):
        odd[p].append(diag_first[g])
        odd[q].append(diag_second[g])
    mom = [diffs[a] + (odd[a][0] + odd[a][1]) for a in range(3)]
    density = f[0] + ((sums[0] + sums[1]) + sums[2]) + ((diag_sum[0] + diag_sum[1]) + diag_sum[2])
    count, held, memory = fields
    force = []
    for a in range(3):
        kept = held[a]
        for weight, earlier in zip(memory, seen_m):
            kept = kept + weight * earlier[a]
        force.append(COUPLING_MASS * (kept - count * mom[a]))
    half = [0.5 * force[a] for a in range(3)]
    vel = [mom[a] + half[a] for a in range(3)]
    press = [mom[a] * mom[a] - half[a] * half[a] for a in range(3)]
    press_sum = press[0] + press[1] + press[2]
    work = [vel[a] * force[a] for a in range(3)]
    work_third = (work[0] + work[1] + work[2]) * (1.0 / 3.0)
    base = density * (1.0 / 9.0) - press_sum * (1.0 / 6.0)
    gaps = []
    for a in range(3):
        gaps.append(base + 0.5 * press[a] - sums[a])
    for g, (p, q, k) in enumerate(DIAGONALS):
        gaps.append(base + 0.5 * (press[p] + press[q]) - diag_sum[g])
    change = []
    for a in range(6):
        total = even_c[a][0] * gaps[0]
        for b in range(1, 6):
            total = total + even_c[a][b] * gaps[b]
        if a < 3:
            total = total + 0.5 * (work[a] - work_third)
        else:
            p, q, k = DIAGONALS[a - 3]
            total = total + 0.25 * (work[p] + work[q] - work_third)
        change.append(total)
    rest = f[0] - 2.0 * (change[0] + change[1] + change[2]) - 4.0 * (change[3] + change[4] + change[5])
    odd_axis, odd_diag = [], []
    for a in range(3):
        third = mom[a] * (1.0 / 3.0)
        g1, g2 = third - odd[a][0], third - odd[a][1]
        d1 = odd_c[a][0][0] * g1 + odd_c[a][0][1] * g2
        d2 = odd_c[a][1][0] * g1 + odd_c[a][1][1] * g2
        push = force[a] * (1.0 / 12.0)
        odd_axis.append(2.0 * (push - (d1 + d2)))
        odd_diag.append([push + d1, push + d2])
    out = [None] * 19
    out[0] = rest
    for a in range(3):
        out[1 + 2 * a] = f[1 + 2 * a] + (change[a] + odd_axis[a])
        out[2 + 2 * a] = f[2 + 2 * a] + (change[a] - odd_axis[a])
    place = [0, 0, 0]
    for g, (p, q, k) in enumerate(DIAGONALS):
        o1, o2 = odd_diag[p][place[p]], odd_diag[q][place[q]]
        place[p] += 1
        place[q] += 1
        gap = mom[p] * mom[q] - half[p] * half[q] - diag_cross[g]
        cross = cross_c[g] * gap + 0.25 * (vel[p] * force[q] + vel[q] * force[p])
        s_plus, s_minus = change[3 + g] + cross, change[3 + g] - cross
        o_plus, o_minus = o1 + o2, o1 - o2
        out[k] = f[k] + (s_plus + o_plus)
        out[k + 1] = f[k + 1] + (s_plus - o_plus)
        out[k + 2] = f[k + 2] + (s_minus + o_minus)
        out[k + 3] = f[k + 3] + (s_minus - o_minus)
    out = [jnp.where(solid, f[OPPOSITE[k]], out[k]) for k in range(19)]
    return out, mom


def kernel(
    dims,
    pop_hbm,
    rates_ref,
    solid_ref,
    dest_ref,
    cell_ref,
    vel_ref,
    coup_ref,
    out_hbm,
    back_out,
    rank_rows,
    pop,
    moved,
    stayed,
    own_hits,
    packing,
    send1,
    recv1,
    send2,
    recv2,
    slots,
    cells,
    weights,
    seen,
    plane_hits,
    slot_hits,
    depth_hits,
    spread,
    summed,
    found_a,
    found_b,
    fields,
    mom,
    mom_t,
    coef_ref,
    pop_sem,
    out_sem,
    a2a_send,
    a2a_recv,
    halo_send,
    halo_recv,
):
    n_chan, n_width, size_x, size_y, size_z, parts = dims
    n_dev = n_chan * n_width
    rows = n_dev * CAP // 128
    planes = size_x * size_y
    chan, width = lax.axis_index("chan"), lax.axis_index("width")
    me = chan * n_width + width
    f32, bf16, i32 = jnp.float32, jnp.bfloat16, jnp.int32

    barrier = pltpu.get_barrier_semaphore()

    def wrap(x, n):
        return jnp.where(x >= n, x - n, x)

    across = [n_width // 2 + (1 - 2 * (j % 2)) * ((j + 1) // 2) for j in range(n_width - 1)] + [0]
    widths = [wrap(width + d, n_width) for d in across]

    def each_peer(act):
        def one(j, _):
            odd = lax.rem(j, 2)
            d = n_chan // 2 + (1 - 2 * odd) * ((j + odd) // 2)
            c = wrap(chan + d, n_chan)
            for w in widths:
                act(c, w)
            return 0

        lax.fori_loop(0, n_chan - 1, one, 0, unroll=3)
        for w in widths[:-1]:
            act(chan, w)

    def greet(c, w):
        pl.semaphore_signal(barrier, inc=1, device_id=(c, w), device_id_type=MESH)

    each_peer(greet)
    pop_copy = pltpu.make_async_copy(pop_hbm, pop, pop_sem)
    pop_copy.start()

    even_table, odd_tables, cross_table = sector_tables()
    rates = [jnp.full((8, 128), rates_ref[j], f32) for j in range(15)]
    places = 0
    for a in range(6):
        for b in range(6):
            coef_ref[places] = weigh(rates, even_table[a, b])
            places += 1
    for axis in range(3):
        for a in range(2):
            for b in range(2):
                coef_ref[places] = weigh(rates, odd_tables[axis][a, b])
                places += 1
    for g in range(3):
        coef_ref[places] = weigh(rates, cross_table[g])
        places += 1

    block = 256
    tri = (
        lax.broadcasted_iota(i32, (block, block), 0) <= lax.broadcasted_iota(i32, (block, block), 1)
    ).astype(f32).astype(bf16)
    dev_iota = lax.broadcasted_iota(i32, (n_dev, block), 0)
    cap_iota = lax.broadcasted_iota(i32, (CAP, block), 0).astype(f32)

    def pack(b, before):
        s = pl.ds(pl.multiple_of(b * block, block), block)
        hits = jnp.where(dev_iota == dest_ref[:, s], 1.0, 0.0)
        hits_b = hits.astype(bf16)
        own_hits[:, s] = hits_b
        upto = dot_nn(hits_b, tri)
        rank = jnp.sum(hits * (upto + before), axis=0, keepdims=True) - 1.0
        rank_rows[:, s] = rank
        rank_hit = cap_iota == rank
        cell = cell_ref[:, s]
        mask = jnp.where(rank_hit, 1.0, 0.0).astype(bf16).reshape(CAP // 16, 16, block)
        pairs = []
        for value in (coup_ref[:, s], vel_ref[0:1, s], vel_ref[1:2, s], vel_ref[2:3, s]):
            pairs.append(split_bf16(jnp.broadcast_to(value, (16, block))))
        order = [pairs[0][0], pairs[1][0], pairs[0][1], pairs[1][1]]
        order += [pairs[2][0], pairs[3][0], pairs[2][1], pairs[3][1]]
        for part in (cell // 128, lax.rem(cell, 128)):
            order.append(jnp.broadcast_to(part.astype(f32), (16, block)).astype(bf16))
        for j, row in enumerate(order):
            packing[j * CAP : (j + 1) * CAP, s] = (mask * row[None]).reshape(CAP, block)
        return before + upto[:, block - 1 : block]

    lax.fori_loop(0, parts // block, pack, jnp.zeros((n_dev, 1), f32), unroll=4)
    packed = dot_nt(own_hits[...], packing[...])
    low = lax.broadcasted_iota(i32, (n_dev, 128), 1) < 64
    send1[0] = packed[:, 0:128] + packed[:, 128:256]
    send1[1] = packed[:, 256:384] + packed[:, 384:512]
    last = packed[:, 512:640]
    send1[2] = jnp.where(low, last * 128.0 + pltpu.roll(last, 64, 1), 0.0)

    pl.semaphore_wait(barrier, n_dev - 1)

    def exchange_send(src, dst, which, c, w):
        o = c * n_width + w
        pltpu.make_async_remote_copy(
            src.at[:, pl.ds(o, 1)],
            dst.at[:, pl.ds(me, 1)],
            a2a_send.at[which],
            a2a_recv.at[which],
            device_id=(c, w),
            device_id_type=MESH,
        ).start()

    def exchange_wait(src, dst, which):
        part = pl.ds(0, n_dev - 1)
        pltpu.make_async_copy(dst.at[:, part], dst.at[:, part], a2a_recv.at[which]).wait()
        pltpu.make_async_copy(src.at[:, part], src.at[:, part], a2a_send.at[which]).wait()

    each_peer(functools.partial(exchange_send, send1, recv1, 0))
    recv1[:, pl.ds(me, 1), :] = send1[:, pl.ds(me, 1), :]
    exchange_wait(send1, recv1, 0)

    half_dev = n_dev // 2
    low = lax.broadcasted_iota(i32, (half_dev, 128), 1) < 64

    def both(ref):
        first, second = ref[0:half_dev, :], ref[half_dev:n_dev, :]
        return (
            jnp.where(low, first, pltpu.roll(second, 64, 1)),
            jnp.where(low, pltpu.roll(first, 64, 1), second),
        )

    coup, vx = both(recv1[0])
    vy, vz = both(recv1[1])
    cell = both(recv1[2])[0].astype(i32)
    slots[0], slots[1], slots[2], slots[3] = coup, vx, vy, vz
    cells[0] = (cell // 128).astype(f32)
    cells[1] = lax.rem(cell, 128).astype(f32)
    weights[0], weights[1], weights[2] = coup * vx, coup * vy, coup * vz
    weights[3] = coup

    plane_iota = lax.broadcasted_iota(i32, (planes, 128), 0).astype(f32).astype(bf16)
    plane_iota = plane_iota.reshape(planes // 16, 16, 128)
    plane_lanes = lax.broadcasted_iota(i32, (128, planes), 1).astype(f32).astype(bf16)
    depth_iota_b = lax.broadcasted_iota(i32, (size_z, 128), 0).astype(f32).astype(bf16)
    depth_iota_b = depth_iota_b.reshape(size_z // 16, 16, 128)
    depth_iota = lax.broadcasted_iota(i32, (size_z, 128), 0).astype(f32)

    one, zero = jnp.bfloat16(1.0), jnp.bfloat16(0.0)

    def row_of(which, i):
        return jnp.broadcast_to(cells[which, pl.ds(i, 1), :], (16, 128)).astype(bf16)[None]

    def place(n):
        columns = cells[0, pl.ds(pl.multiple_of(8 * n, 8), 8), :].T
        for r in range(8):
            i = 8 * n + r
            s = pl.ds(pl.multiple_of(i * 128, 128), 128)
            hits = jnp.where(plane_iota == row_of(0, i), one, zero).reshape(planes, 128)
            plane_hits[0:planes, s] = hits
            plane_hits[planes : 2 * planes, s] = hits
            hits = jnp.where(depth_iota_b == row_of(1, i), one, zero).reshape(size_z, 128)
            depth_hits[:, s] = hits
            column = jnp.broadcast_to(columns[:, r : r + 1], (128, planes)).astype(bf16)
            slot_hits[s, :] = jnp.where(plane_lanes == column, one, zero)

    chunk = 1024
    chunk_rows = chunk // 128

    chunks = rows // chunk_rows
    pieces = min(PIECES, chunks)

    def weigh_chunk(n, spread):
        for r in range(chunk_rows):
            i = n * chunk_rows + r
            hits = depth_hits[:, pl.ds(pl.multiple_of(i * 128, 128), 128)]
            hits = hits.reshape(size_z // 16, 16, 128)
            for j in range(4):
                value = jnp.broadcast_to(weights[j, pl.ds(i, 1), :], (16, 128))
                for h, piece in enumerate(split_bf16(value)):
                    at = (2 * j + h) * size_z
                    spread[at : at + size_z, r * 128 : (r + 1) * 128] = (
                        hits * piece[None]
                    ).reshape(size_z, 128)

    def add_chunk(n, spread):
        s = pl.ds(pl.multiple_of(n * chunk, chunk), chunk)
        summed[...] += dot_nn(spread[...], slot_hits[s, :])

    def ends_first(i):
        return jnp.where(i == 0, 0, jnp.where(i == 1, size_x - 1, i - 1))

    def scatter(targets, before=None, beside=None, early=None):
        summed[...] = jnp.zeros_like(summed)
        share = size_x // chunks

        def some(n, _):
            for part in range(pieces):
                p = pieces * n + part
                if before is not None:
                    before(p)
                weigh_chunk(p, spread.at[part])
                add_chunk(p, spread.at[part])
                if beside is not None:
                    for i in range(share):
                        beside(ends_first(p * share + i))
            if early is not None:

                @pl.when(n == 0)
                def _():
                    early()

            return 0

        lax.fori_loop(0, chunks // pieces, some, 0)
        for j, target in enumerate(targets):
            at = 2 * j * size_z
            total = summed[at : at + size_z, :] + summed[at + size_z : at + 2 * size_z, :]
            fields[target] = total.T

    tile = min(1024, rows * 128 // 2)
    tile_rows = tile // 128

    def find(n, found):
        s = pl.ds(pl.multiple_of(n * tile, tile), tile)
        found[...] = dot_nn(mom_t[...], plane_hits[:, s])

    def pick(n, found):
        for r in range(tile_rows):
            i = n * tile_rows + r
            hit = depth_iota == cells[1, pl.ds(i, 1), :]
            for a in range(3):
                both = found[a * size_z : (a + 1) * size_z, r * 128 : (r + 1) * 128]
                seen[a, pl.ds(i, 1), :] = jnp.sum(
                    jnp.where(hit, both, 0.0), axis=0, keepdims=True
                )

    tiles = rows // tile_rows
    first_tile = lax.rem(me, rows) // tile_rows

    def gather(t, then=None):
        for a in range(3):
            hi, lo = split_bf16(mom[t, a].T)
            mom_t[a * size_z : (a + 1) * size_z, 0:planes] = hi
            mom_t[a * size_z : (a + 1) * size_z, planes : 2 * planes] = lo

        def turn(n):
            return n if then is None else lax.rem(n + first_tile, tiles)

        def use(n, found, own=False):
            pick(turn(n), found)
            if then is not None:
                then(turn(n), own)

        find(turn(0), found_a)
        find(turn(1), found_b)
        use(0, found_a, True)

        def two(n, _):
            find(turn(2 * n + 2), found_a)
            use(2 * n + 1, found_b)
            find(turn(2 * n + 3), found_b)
            use(2 * n + 2, found_a)
            return 0

        lax.fori_loop(0, tiles // 2 - 1, two, 0)
        use(tiles - 1, found_b)
        if then is None:
            for a in range(3):
                slots[1 + a] = slots[1 + a] + slots[0] * (seen[a] - slots[1 + a])

    def deliver(n, own):
        s = pl.ds(pl.multiple_of(n * tile_rows, tile_rows), tile_rows)
        upper = pl.ds(pl.multiple_of(half_dev + n * tile_rows, tile_rows), tile_rows)
        low = lax.broadcasted_iota(i32, (tile_rows, 128), 1) < 64
        c = slots[0, s, :]
        vx, vy, vz = [
            slots[1 + a, s, :] + c * (seen[a, s, :] - slots[1 + a, s, :]) for a in range(3)
        ]
        send2[0, s, :] = jnp.where(low, vx, pltpu.roll(vy, 64, 1))
        send2[0, upper, :] = jnp.where(low, pltpu.roll(vx, 64, 1), vy)
        send2[1, s, :] = jnp.where(low, vz, 0.0)
        send2[1, upper, :] = jnp.where(low, pltpu.roll(vz, 64, 1), 0.0)
        for r in range(tile_rows):
            for side in range(2):
                c = (side * half_dev + r) // n_width + n * (tile_rows // n_width)
                w = r % n_width

                if own:

                    @pl.when(jnp.logical_or(c != chan, w != width))
                    def _():
                        exchange_send(send2, recv2, 1, c, w)

                else:
                    exchange_send(send2, recv2, 1, c, w)

    def nb(dc, dw):
        return (lax.rem(chan + dc + n_chan, n_chan), lax.rem(width + dw + n_width, n_width))

    inner_x, inner_y = pl.ds(1, size_x), pl.ds(PAD, size_y)
    last_x, last_y = size_x, PAD + size_y - 1
    end_x, end_y = size_x + 1, PAD + size_y

    def halo_copy(t, n):
        g = moved.at[t % 2]
        parts_list = [
            (g.at[0:5, last_x, inner_y], g.at[0:5, 0, inner_y], nb(1, 0)),
            (g.at[8:13, 1, inner_y], g.at[8:13, end_x, inner_y], nb(-1, 0)),
            (g.at[4:9, inner_x, last_y], g.at[4:9, inner_x, PAD - 1], nb(0, 1)),
            (g.at[12:16, inner_x, PAD], g.at[12:16, inner_x, end_y], nb(0, -1)),
            (g.at[0:1, inner_x, PAD], g.at[0:1, inner_x, end_y], nb(0, -1)),
            (g.at[4, last_x, pl.ds(last_y, 1)], g.at[4, 0, pl.ds(PAD - 1, 1)], nb(1, 1)),
            (g.at[12, 1, pl.ds(PAD, 1)], g.at[12, end_x, pl.ds(end_y, 1)], nb(-1, -1)),
            (g.at[0, last_x, pl.ds(PAD, 1)], g.at[0, 0, pl.ds(end_y, 1)], nb(1, -1)),
            (g.at[8, 1, pl.ds(last_y, 1)], g.at[8, end_x, pl.ds(PAD - 1, 1)], nb(-1, 1)),
        ]
        src, dst, to = parts_list[n]
        return pltpu.make_async_remote_copy(
            src, dst, halo_send.at[t, n], halo_recv.at[t, n], device_id=to, device_id_type=MESH
        )

    def load(t, i, h):
        f = []
        for k in range(19):
            if t == 0:
                f.append(pop[k, i, 8 * h : 8 * h + 8, :])
            elif k in STAY:
                f.append(stayed[(t - 1) % 2, STAY[k], i, 8 * h : 8 * h + 8, :])
            else:
                step_x, step_y, _ = LATTICE[k]
                start = PAD + 8 * h - step_y
                f.append(moved[(t - 1) % 2, SLOT_OF[k], i + 1 - step_x, start : start + 8, :])
        return f

    def step_plane(t):
        def one(i):
            coef = [coef_ref[n] for n in range(51)]
            even_c = [coef[6 * a : 6 * a + 6] for a in range(6)]
            odd_c = [
                [coef[36 + 4 * a : 38 + 4 * a], coef[38 + 4 * a : 40 + 4 * a]] for a in range(3)
            ]
            coefs = (even_c, odd_c, coef[48:51])
            for h in range(size_y // 8):
                f = load(t, i, h)
                at = pl.ds(pl.multiple_of(i * size_y + 8 * h, 8), 8)
                count = fields[0, at, :]
                held = [fields[1 + 3 * (t % 2) + a, at, :] for a in range(3)]
                memory = [fields[7 + t - 1 - s, at, :] for s in range(t)]
                seen_m = [[mom[s, a, at, :] for a in range(3)] for s in range(t)]
                solid = solid_ref[i, 8 * h : 8 * h + 8, :] == 1
                out, m = relax_group(f, (count, held, memory), seen_m, solid, coefs)
                for a in range(3):
                    mom[t, a, at, :] = m[a]
                for k in range(19):
                    value = out[k]
                    if LATTICE[k][2]:
                        value = pltpu.roll(value, LATTICE[k][2] % size_z, 1)
                    if k in STAY:
                        stayed[t % 2, STAY[k], i, 8 * h : 8 * h + 8, :] = value
                    else:
                        moved[t % 2, SLOT_OF[k], i + 1, PAD + 8 * h : PAD + 8 * h + 8, :] = value

        return one

    scatter([1, 2, 3, 0], before=place)
    coup = slots[0]
    keep = 1.0 - coup
    weights[3] = coup * coup
    pop_copy.wait()
    for t in range(STEPS):
        plane = step_plane(t)

        def send_ends():
            for n in (5, 6, 7, 8, 0, 1):
                halo_copy(t, n).start()

        if t < STEPS - 1:
            for a in range(3):
                weights[a] = weights[a] * keep
            if t > 0:
                weights[3] = weights[3] * keep
            odd = (t + 1) % 2
            scatter([1 + 3 * odd, 2 + 3 * odd, 3 + 3 * odd, 7 + t], None, plane, send_ends)
        else:

            def one(i, _):
                plane(i)
                return 0

            plane(0)
            plane(size_x - 1)
            send_ends()
            lax.fori_loop(1, size_x - 1, one, 0, unroll=2)
        for n in (2, 3, 4):
            halo_copy(t, n).start()
        if t < STEPS - 1:
            gather(t)
        else:
            gather(t, deliver)
        for n in range(9):
            halo_copy(t, n).wait()

    def finish(i, _):
        for h in range(size_y // 8):
            f = load(STEPS, i, h)
            for k in range(19):
                pop[k, i, 8 * h : 8 * h + 8, :] = f[k]
        return 0

    lax.fori_loop(0, size_x, finish, 0)
    out_copy = pltpu.make_async_copy(pop, out_hbm, out_sem)
    out_copy.start()
    recv2[:, pl.ds(me, 1), :] = send2[:, pl.ds(me, 1), :]
    exchange_wait(send2, recv2, 1)

    back_out[...] = recv2[...]
    out_copy.wait()


def finish_kernel(dims, pop_hbm, back_ref, dest_ref, rank_ref, out_hbm, vel_out, held, sems):
    n_dev, parts = dims
    f32, bf16, i32 = jnp.float32, jnp.bfloat16, jnp.int32
    copies_in = [pltpu.make_async_copy(pop_hbm.at[k], held.at[k], sems.at[0, k]) for k in range(19)]
    copies_out = [
        pltpu.make_async_copy(held.at[k], out_hbm.at[k], sems.at[1, k]) for k in range(19)
    ]
    for copy in copies_in:
        copy.start()
    block = min(1024, parts)
    dev_iota = lax.broadcasted_iota(i32, (n_dev, block), 0)
    cap_iota = lax.broadcasted_iota(i32, (CAP, block), 0).astype(f32)
    back = [split_bf16(back_ref[a].T) for a in range(2)]
    back = jnp.concatenate([back[0][0], back[1][0][0:64], back[0][1], back[1][1][0:64]], axis=0)

    def unpack(b, _):
        s = pl.ds(pl.multiple_of(b * block, block), block)
        hits = jnp.where(dev_iota == dest_ref[:, s], 1.0, 0.0).astype(bf16)
        found = dot_nn(back, hits)
        hit = cap_iota == rank_ref[:, s]
        for a in range(3):
            value = found[64 * a : 64 * a + 64] + found[64 * (a + 3) : 64 * (a + 3) + 64]
            vel_out[a : a + 1, s] = jnp.sum(jnp.where(hit, value, 0.0), axis=0, keepdims=True)
        return 0

    blocks = parts // block
    lax.fori_loop(0, blocks // 4, unpack, 0)
    for arrived, leaving in zip(copies_in, copies_out):
        arrived.wait()
        leaving.start()
    lax.fori_loop(blocks // 4, blocks, unpack, 0)
    for copy in copies_out:
        copy.wait()


def per_device(
    n_chan,
    n_width,
    populations,
    moment_rates,
    solid_flags,
    destination,
    local_cell,
    particle_velocity,
    coupling,
):
    _, size_x, size_y, size_z = populations.shape
    parts = destination.shape[0]
    n_dev = n_chan * n_width
    rows = n_dev * CAP // 128
    planes = size_x * size_y
    f32, bf16 = jnp.float32, jnp.bfloat16
    vmem = pl.BlockSpec(memory_space=pltpu.VMEM)
    chunk = 1024
    tile = min(1024, rows * 128 // 2)
    destination = destination.reshape(1, parts)
    moved, back, ranks = pl.pallas_call(
        functools.partial(kernel, (n_chan, n_width, size_x, size_y, size_z, parts)),
        out_shape=(
            jax.ShapeDtypeStruct(populations.shape, f32),
            jax.ShapeDtypeStruct((2, n_dev, 128), f32),
            jax.ShapeDtypeStruct((1, parts), f32),
        ),
        in_specs=[
            pl.BlockSpec(memory_space=pl.ANY),
            pl.BlockSpec(memory_space=pltpu.SMEM),
            vmem,
            vmem,
            vmem,
            vmem,
            vmem,
        ],
        out_specs=(pl.BlockSpec(memory_space=pl.ANY), vmem, vmem),
        scratch_shapes=[
            pltpu.VMEM(populations.shape, f32),
            pltpu.VMEM((2, 16, size_x + 2, size_y + 2 * PAD, size_z), f32),
            pltpu.VMEM((2, 3, size_x, size_y, size_z), f32),
            pltpu.VMEM((n_dev, parts), bf16),
            pltpu.VMEM((10 * CAP, parts), bf16),
            pltpu.VMEM((3, n_dev, 128), f32),
            pltpu.VMEM((3, n_dev, 128), f32),
            pltpu.VMEM((2, n_dev, 128), f32),
            pltpu.VMEM((2, n_dev, 128), f32),
            pltpu.VMEM((4, rows, 128), f32),
            pltpu.VMEM((2, rows, 128), f32),
            pltpu.VMEM((4, rows, 128), f32),
            pltpu.VMEM((3, rows, 128), f32),
            pltpu.VMEM((2 * planes, rows * 128), bf16),
            pltpu.VMEM((rows * 128, planes), bf16),
            pltpu.VMEM((size_z, rows * 128), bf16),
            pltpu.VMEM((PIECES, 8 * size_z, chunk), bf16),
            pltpu.VMEM((8 * size_z, planes), f32),
            pltpu.VMEM((3 * size_z, tile), f32),
            pltpu.VMEM((3 * size_z, tile), f32),
            pltpu.VMEM((10, planes, size_z), f32),
            pltpu.VMEM((STEPS, 3, planes, size_z), f32),
            pltpu.VMEM((3 * size_z, 2 * planes), bf16),
            pltpu.VMEM((51, 8, 128), f32),
            pltpu.SemaphoreType.DMA,
            pltpu.SemaphoreType.DMA,
            pltpu.SemaphoreType.DMA((2,)),
            pltpu.SemaphoreType.DMA((2,)),
            pltpu.SemaphoreType.DMA((STEPS, 9)),
            pltpu.SemaphoreType.DMA((STEPS, 9)),
        ],
        compiler_params=pltpu.CompilerParams(
            collective_id=0, has_side_effects=True, vmem_limit_bytes=56 * 1024 * 1024
        ),
        name="lattice_steps",
    )(
        populations,
        moment_rates,
        solid_flags,
        destination,
        local_cell.reshape(1, parts),
        particle_velocity,
        coupling.reshape(1, parts),
    )
    return pl.pallas_call(
        functools.partial(finish_kernel, (n_dev, parts)),
        out_shape=(
            jax.ShapeDtypeStruct(populations.shape, f32),
            jax.ShapeDtypeStruct(particle_velocity.shape, f32),
        ),
        in_specs=[pl.BlockSpec(memory_space=pl.ANY), vmem, vmem, vmem],
        out_specs=(pl.BlockSpec(memory_space=pl.ANY), vmem),
        scratch_shapes=[
            pltpu.VMEM(populations.shape, f32),
            pltpu.SemaphoreType.DMA((2, 19)),
        ],
        compiler_params=pltpu.CompilerParams(vmem_limit_bytes=56 * 1024 * 1024),
        name="particles_back",
    )(moved, back, destination, ranks)


def solution(mesh):
    return jax.shard_map(
        functools.partial(per_device, mesh.shape["chan"], mesh.shape["width"]),
        mesh=mesh,
        in_specs=(
            P(None, "chan", "width", None),
            P(),
            P("chan", "width", None),
            P(("chan", "width"), None),
            P(("chan", "width")),
            P(None, ("chan", "width")),
            P(("chan", "width")),
        ),
        out_specs=(P(None, "chan", "width", None), P(None, ("chan", "width"))),
        check_vma=False,
    )
```

```python
import functools
import math

import jax
import jax.numpy as jnp
import numpy as np
from jax import lax
from jax.experimental import pallas as pl
from jax.experimental.pallas import tpu as pltpu
from jax.sharding import PartitionSpec as P

MESH = pl.DeviceIdType.MESH
STEPS = 4
CAP = 64
PIECES = 4
LATTICE = [
    [0, 0, 0],
    [1, 0, 0],
    [-1, 0, 0],
    [0, 1, 0],
    [0, -1, 0],
    [0, 0, 1],
    [0, 0, -1],
    [1, 1, 0],
    [-1, -1, 0],
    [1, -1, 0],
    [-1, 1, 0],
    [1, 0, 1],
    [-1, 0, -1],
    [1, 0, -1],
    [-1, 0, 1],
    [0, 1, 1],
    [0, -1, -1],
    [0, 1, -1],
    [0, -1, 1],
]
OPPOSITE = [0, 2, 1, 4, 3, 6, 5, 8, 7, 10, 9, 12, 11, 14, 13, 16, 15, 18, 17]
COUPLING_MASS = 0.02
RING = [9, 1, 11, 13, 7, 3, 15, 17, 10, 2, 12, 14, 8, 4, 16, 18]
SLOT_OF = {k: i for i, k in enumerate(RING)}
STAY = {0: 0, 5: 1, 6: 2}
PAD = 8
DIAGONALS = [(0, 1, 7), (0, 2, 11), (1, 2, 15)]


def moment_basis():
    lattice_np = np.array(LATTICE, dtype=np.float32)
    along_x, along_y, along_z = (lattice_np[:, 0], lattice_np[:, 1], lattice_np[:, 2])
    columns = [
        np.ones(19, dtype=np.float32),
        along_x,
        along_y,
        along_z,
        along_x * along_x,
        along_y * along_y,
        along_z * along_z,
        along_x * along_y,
        along_x * along_z,
        along_y * along_z,
        along_x * along_y * along_y,
        along_x * along_z * along_z,
        along_y * along_x * along_x,
        along_y * along_z * along_z,
        along_z * along_x * along_x,
        along_z * along_y * along_y,
        along_x * along_x * along_y * along_y,
        along_x * along_x * along_z * along_z,
        along_y * along_y * along_z * along_z,
    ]
    found_cols = []
    for column in columns:
        vector = np.array(column, dtype=np.float32)
        for repeat_pass in range(2):
            for earlier in found_cols:
                vector = vector - float(np.dot(earlier, vector)) * earlier
        found_cols.append((vector / math.sqrt(float(np.dot(vector, vector)))).astype(np.float32))
    return np.stack(found_cols[4:], axis=1).astype(np.float32)


def sector_tables():
    basis = moment_basis().astype(np.float64)

    def vec(entries):
        v = np.zeros(19)
        for k, s in entries:
            v[k] = s
        return v

    def project(members):
        m = np.stack(members)
        dots = m @ basis
        dots[np.abs(dots) < 1e-5] = 0.0
        sizes = np.sum(np.abs(m), axis=1)
        return dots[:, None, :] * dots[None, :, :] / sizes[None, :, None]

    even = [vec([(0, 1)])]
    for a in range(3):
        even.append(vec([(1 + 2 * a, 1), (2 + 2 * a, 1)]))
    for a, b, k in DIAGONALS:
        even.append(vec([(k + i, 1) for i in range(4)]))
    table = project(even)
    table = table[1:, 1:] - table[1:, :1]
    table[:3] *= 0.5
    table[3:] *= 0.25
    even_table = table
    odd_tables = []
    for a in range(3):
        members = [vec([(1 + 2 * a, 1), (2 + 2 * a, -1)])]
        for p, q, k in DIAGONALS:
            if a in (p, q):
                members.append(vec([(k + i, LATTICE[k + i][a]) for i in range(4)]))
        table = project(members)
        odd_tables.append((table[1:, 1:] - table[1:, :1]) * 0.25)
    cross = []
    for p, q, k in DIAGONALS:
        table = project([vec([(k + i, LATTICE[k + i][p] * LATTICE[k + i][q]) for i in range(4)])])
        cross.append(table[0, 0] * 0.25)
    return even_table, odd_tables, cross


def weigh(rates, weights):
    total = None
    for j in range(15):
        if abs(weights[j]) > 1e-9:
            term = rates[j] * float(weights[j])
            total = term if total is None else total + term
    return total if total is not None else jnp.zeros_like(rates[0])


def split_bf16(x):
    hi = x.astype(jnp.bfloat16)
    lo = (x - hi.astype(jnp.float32)).astype(jnp.bfloat16)
    return hi, lo


def dot_nt(a, b):
    return lax.dot_general(a, b, (((1,), (1,)), ((), ())), preferred_element_type=jnp.float32)


def dot_nn(a, b):
    return lax.dot_general(a, b, (((1,), (0,)), ((), ())), preferred_element_type=jnp.float32)


def relax_group(f, fields, seen_m, solid, coef):
    even_c, odd_c, cross_c = coef
    sums, diffs = [], []
    for a in range(3):
        p, n = f[1 + 2 * a], f[2 + 2 * a]
        sums.append(p + n)
        diffs.append(p - n)
    diag_sum, diag_cross, diag_first, diag_second = [], [], [], []
    for p, q, k in DIAGONALS:
        a1, b1 = f[k] + f[k + 1], f[k] - f[k + 1]
        a2, b2 = f[k + 2] + f[k + 3], f[k + 2] - f[k + 3]
        diag_sum.append(a1 + a2)
        diag_cross.append(a1 - a2)
        diag_first.append(b1 + b2)
        diag_second.append(b1 - b2)
    odd = [[], [], []]
    for g, (p, q, k) in enumerate(DIAGONALS):
        odd[p].append(diag_first[g])
        odd[q].append(diag_second[g])
    mom = [diffs[a] + (odd[a][0] + odd[a][1]) for a in range(3)]
    density = f[0] + ((sums[0] + sums[1]) + sums[2]) + ((diag_sum[0] + diag_sum[1]) + diag_sum[2])
    count, held, memory = fields
    force = []
    for a in range(3):
        kept = held[a]
        for weight, earlier in zip(memory, seen_m):
            kept = kept + weight * earlier[a]
        force.append(COUPLING_MASS * (kept - count * mom[a]))
    half = [0.5 * force[a] for a in range(3)]
    vel = [mom[a] + half[a] for a in range(3)]
    press = [mom[a] * mom[a] - half[a] * half[a] for a in range(3)]
    press_sum = press[0] + press[1] + press[2]
    work = [vel[a] * force[a] for a in range(3)]
    work_third = (work[0] + work[1] + work[2]) * (1.0 / 3.0)
    base = density * (1.0 / 9.0) - press_sum * (1.0 / 6.0)
    gaps = []
    for a in range(3):
        gaps.append(base + 0.5 * press[a] - sums[a])
    for g, (p, q, k) in enumerate(DIAGONALS):
        gaps.append(base + 0.5 * (press[p] + press[q]) - diag_sum[g])
    change = []
    for a in range(6):
        total = even_c[a][0] * gaps[0]
        for b in range(1, 6):
            total = total + even_c[a][b] * gaps[b]
        if a < 3:
            total = total + 0.5 * (work[a] - work_third)
        else:
            p, q, k = DIAGONALS[a - 3]
            total = total + 0.25 * (work[p] + work[q] - work_third)
        change.append(total)
    rest = f[0] - 2.0 * (change[0] + change[1] + change[2]) - 4.0 * (change[3] + change[4] + change[5])
    odd_axis, odd_diag = [], []
    for a in range(3):
        third = mom[a] * (1.0 / 3.0)
        g1, g2 = third - odd[a][0], third - odd[a][1]
        d1 = odd_c[a][0][0] * g1 + odd_c[a][0][1] * g2
        d2 = odd_c[a][1][0] * g1 + odd_c[a][1][1] * g2
        push = force[a] * (1.0 / 12.0)
        odd_axis.append(2.0 * (push - (d1 + d2)))
        odd_diag.append([push + d1, push + d2])
    out = [None] * 19
    out[0] = rest
    for a in range(3):
        out[1 + 2 * a] = f[1 + 2 * a] + (change[a] + odd_axis[a])
        out[2 + 2 * a] = f[2 + 2 * a] + (change[a] - odd_axis[a])
    place = [0, 0, 0]
    for g, (p, q, k) in enumerate(DIAGONALS):
        o1, o2 = odd_diag[p][place[p]], odd_diag[q][place[q]]
        place[p] += 1
        place[q] += 1
        gap = mom[p] * mom[q] - half[p] * half[q] - diag_cross[g]
        cross = cross_c[g] * gap + 0.25 * (vel[p] * force[q] + vel[q] * force[p])
        s_plus, s_minus = change[3 + g] + cross, change[3 + g] - cross
        o_plus, o_minus = o1 + o2, o1 - o2
        out[k] = f[k] + (s_plus + o_plus)
        out[k + 1] = f[k + 1] + (s_plus - o_plus)
        out[k + 2] = f[k + 2] + (s_minus + o_minus)
        out[k + 3] = f[k + 3] + (s_minus - o_minus)
    out = [jnp.where(solid, f[OPPOSITE[k]], out[k]) for k in range(19)]
    return out, mom


def kernel(
    dims,
    pop_hbm,
    rates_ref,
    solid_hbm,
    dest_hbm,
    cell_hbm,
    vel_hbm,
    coup_hbm,
    out_hbm,
    back_out,
    rank_rows,
    pop,
    solid_ref,
    dest_ref,
    cell_ref,
    vel_ref,
    coup_ref,
    moved_even,
    moved_odd,
    stayed_even,
    stayed_odd,
    own_hits,
    packing,
    send1,
    recv1,
    send2,
    recv2,
    slots,
    cells,
    weights,
    seen,
    plane_hits,
    slot_hits,
    depth_hits,
    spread,
    summed,
    found_a,
    found_b,
    fields,
    mom_0,
    mom_1,
    mom_2,
    mom_3,
    mom_t,
    coef_ref,
    pop_sem,
    in_sems,
    out_sem,
    a2a_send,
    a2a_recv,
    halo_send,
    halo_recv,
):
    n_chan, n_width, size_x, size_y, size_z, parts = dims
    n_dev = n_chan * n_width
    rows = n_dev * CAP // 128
    planes = size_x * size_y
    chan, width = lax.axis_index("chan"), lax.axis_index("width")
    me = chan * n_width + width
    f32, bf16, i32 = jnp.float32, jnp.bfloat16, jnp.int32

    moved, stayed = (moved_even, moved_odd), (stayed_even, stayed_odd)
    mom = (mom_0, mom_1, mom_2, mom_3)
    small = [(dest_hbm, dest_ref), (cell_hbm, cell_ref), (vel_hbm, vel_ref), (coup_hbm, coup_ref)]
    small.append((solid_hbm, solid_ref))
    small = [pltpu.make_async_copy(a, b, in_sems.at[n]) for n, (a, b) in enumerate(small)]
    for copy in small:
        copy.start()
    pop_copy = pltpu.make_async_copy(pop_hbm, pop, pop_sem)
    pop_copy.start()

    barrier = pltpu.get_barrier_semaphore()

    def wrap(x, n):
        return jnp.where(x >= n, x - n, x)

    across = [n_width // 2 + (1 - 2 * (j % 2)) * ((j + 1) // 2) for j in range(n_width - 1)] + [0]
    widths = [wrap(width + d, n_width) for d in across]

    def each_peer(act):
        def one(j, _):
            odd = lax.rem(j, 2)
            d = n_chan // 2 + (1 - 2 * odd) * ((j + odd) // 2)
            c = wrap(chan + d, n_chan)
            for w in widths:
                act(c, w)
            return 0

        lax.fori_loop(0, n_chan - 1, one, 0, unroll=3)
        for w in widths[:-1]:
            act(chan, w)

    def greet(c, w):
        pl.semaphore_signal(barrier, inc=1, device_id=(c, w), device_id_type=MESH)

    each_peer(greet)

    even_table, odd_tables, cross_table = sector_tables()
    rates = [jnp.full((8, 128), rates_ref[j], f32) for j in range(15)]
    places = 0
    for a in range(6):
        for b in range(6):
            coef_ref[places] = weigh(rates, even_table[a, b])
            places += 1
    for axis in range(3):
        for a in range(2):
            for b in range(2):
                coef_ref[places] = weigh(rates, odd_tables[axis][a, b])
                places += 1
    for g in range(3):
        coef_ref[places] = weigh(rates, cross_table[g])
        places += 1

    for copy in small[:4]:
        copy.wait()
    block = 256
    tri = (
        lax.broadcasted_iota(i32, (block, block), 0) <= lax.broadcasted_iota(i32, (block, block), 1)
    ).astype(f32).astype(bf16)
    dev_iota = lax.broadcasted_iota(i32, (n_dev, block), 0)
    cap_iota = lax.broadcasted_iota(i32, (CAP, block), 0).astype(f32)

    def pack(b, before):
        s = pl.ds(pl.multiple_of(b * block, block), block)
        hits = jnp.where(dev_iota == dest_ref[:, s], 1.0, 0.0)
        hits_b = hits.astype(bf16)
        own_hits[:, s] = hits_b
        upto = dot_nn(hits_b, tri)
        rank = jnp.sum(hits * (upto + before), axis=0, keepdims=True) - 1.0
        rank_rows[:, s] = rank
        rank_hit = cap_iota == rank
        cell = cell_ref[:, s]
        mask = jnp.where(rank_hit, 1.0, 0.0).astype(bf16).reshape(CAP // 16, 16, block)
        pairs = []
        for value in (coup_ref[:, s], vel_ref[0:1, s], vel_ref[1:2, s], vel_ref[2:3, s]):
            pairs.append(split_bf16(jnp.broadcast_to(value, (16, block))))
        order = [pairs[0][0], pairs[1][0], pairs[0][1], pairs[1][1]]
        order += [pairs[2][0], pairs[3][0], pairs[2][1], pairs[3][1]]
        for part in (cell // 128, lax.rem(cell, 128)):
            order.append(jnp.broadcast_to(part.astype(f32), (16, block)).astype(bf16))
        for j, row in enumerate(order):
            packing[j * CAP : (j + 1) * CAP, s] = (mask * row[None]).reshape(CAP, block)
        return before + upto[:, block - 1 : block]

    lax.fori_loop(0, parts // block, pack, jnp.zeros((n_dev, 1), f32), unroll=4)
    packed = dot_nt(own_hits[...], packing[...])
    low = lax.broadcasted_iota(i32, (n_dev, 128), 1) < 64
    send1[0] = packed[:, 0:128] + packed[:, 128:256]
    send1[1] = packed[:, 256:384] + packed[:, 384:512]
    last = packed[:, 512:640]
    send1[2] = jnp.where(low, last * 128.0 + pltpu.roll(last, 64, 1), 0.0)

    pl.semaphore_wait(barrier, n_dev - 1)

    def exchange_send(src, dst, which, c, w):
        o = c * n_width + w
        pltpu.make_async_remote_copy(
            src.at[:, pl.ds(o, 1)],
            dst.at[:, pl.ds(me, 1)],
            a2a_send.at[which],
            a2a_recv.at[which],
            device_id=(c, w),
            device_id_type=MESH,
        ).start()

    def exchange_wait(src, dst, which):
        part = pl.ds(0, n_dev - 1)
        pltpu.make_async_copy(dst.at[:, part], dst.at[:, part], a2a_recv.at[which]).wait()
        pltpu.make_async_copy(src.at[:, part], src.at[:, part], a2a_send.at[which]).wait()

    each_peer(functools.partial(exchange_send, send1, recv1, 0))
    recv1[:, pl.ds(me, 1), :] = send1[:, pl.ds(me, 1), :]
    exchange_wait(send1, recv1, 0)

    half_dev = n_dev // 2
    low = lax.broadcasted_iota(i32, (half_dev, 128), 1) < 64

    def both(ref):
        first, second = ref[0:half_dev, :], ref[half_dev:n_dev, :]
        return (
            jnp.where(low, first, pltpu.roll(second, 64, 1)),
            jnp.where(low, pltpu.roll(first, 64, 1), second),
        )

    coup, vx = both(recv1[0])
    vy, vz = both(recv1[1])
    cell = both(recv1[2])[0].astype(i32)
    slots[0], slots[1], slots[2], slots[3] = coup, vx, vy, vz
    cells[0] = (cell // 128).astype(f32)
    cells[1] = lax.rem(cell, 128).astype(f32)
    weights[0], weights[1], weights[2] = coup * vx, coup * vy, coup * vz
    weights[3] = coup

    plane_iota = lax.broadcasted_iota(i32, (planes, 128), 0).astype(f32).astype(bf16)
    plane_iota = plane_iota.reshape(planes // 16, 16, 128)
    plane_lanes = lax.broadcasted_iota(i32, (128, planes), 1).astype(f32).astype(bf16)
    depth_iota_b = lax.broadcasted_iota(i32, (size_z, 128), 0).astype(f32).astype(bf16)
    depth_iota_b = depth_iota_b.reshape(size_z // 16, 16, 128)
    depth_iota = lax.broadcasted_iota(i32, (size_z, 128), 0).astype(f32)

    one, zero = jnp.bfloat16(1.0), jnp.bfloat16(0.0)

    def row_of(which, i):
        return jnp.broadcast_to(cells[which, pl.ds(i, 1), :], (16, 128)).astype(bf16)[None]

    def place(n):
        columns = cells[0, pl.ds(pl.multiple_of(8 * n, 8), 8), :].T
        for r in range(8):
            i = 8 * n + r
            s = pl.ds(pl.multiple_of(i * 128, 128), 128)
            hits = jnp.where(plane_iota == row_of(0, i), one, zero).reshape(planes, 128)
            plane_hits[0:planes, s] = hits
            plane_hits[planes : 2 * planes, s] = hits
            hits = jnp.where(depth_iota_b == row_of(1, i), one, zero).reshape(size_z, 128)
            depth_hits[:, s] = hits
            column = jnp.broadcast_to(columns[:, r : r + 1], (128, planes)).astype(bf16)
            slot_hits[s, :] = jnp.where(plane_lanes == column, one, zero)

    chunk = 1024
    chunk_rows = chunk // 128

    chunks = rows // chunk_rows
    pieces = min(PIECES, chunks)

    def weigh_chunk(n, spread):
        for r in range(chunk_rows):
            i = n * chunk_rows + r
            hits = depth_hits[:, pl.ds(pl.multiple_of(i * 128, 128), 128)]
            hits = hits.reshape(size_z // 16, 16, 128)
            for j in range(4):
                value = jnp.broadcast_to(weights[j, pl.ds(i, 1), :], (16, 128))
                for h, piece in enumerate(split_bf16(value)):
                    at = (2 * j + h) * size_z
                    spread[at : at + size_z, r * 128 : (r + 1) * 128] = (
                        hits * piece[None]
                    ).reshape(size_z, 128)

    def add_chunk(n, spread):
        s = pl.ds(pl.multiple_of(n * chunk, chunk), chunk)
        summed[...] += dot_nn(spread[...], slot_hits[s, :])

    def ends_first(i):
        return jnp.where(i == 0, 0, jnp.where(i == 1, size_x - 1, i - 1))

    def scatter(targets, before=None, beside=None, early=None, late=None):
        summed[...] = jnp.zeros_like(summed)
        share = size_x // chunks

        def some(n, _):
            for part in range(pieces):
                p = pieces * n + part
                if before is not None:
                    before(p)
                weigh_chunk(p, spread.at[part])
                add_chunk(p, spread.at[part])
                if beside is not None:
                    for i in range(share):
                        beside(ends_first(p * share + i))
            if early is not None:

                @pl.when(n == 0)
                def _():
                    early()

            return 0

        lax.fori_loop(0, chunks // pieces, some, 0)
        if late is not None:
            late()
        for j, target in enumerate(targets):
            at = 2 * j * size_z
            total = summed[at : at + size_z, :] + summed[at + size_z : at + 2 * size_z, :]
            fields[target] = total.T

    tile = min(1024, rows * 128 // 2)
    tile_rows = tile // 128

    def find(n, found):
        s = pl.ds(pl.multiple_of(n * tile, tile), tile)
        found[...] = dot_nn(mom_t[...], plane_hits[:, s])

    def pick(n, found):
        for r in range(tile_rows):
            i = n * tile_rows + r
            hit = depth_iota == cells[1, pl.ds(i, 1), :]
            for a in range(3):
                both = found[a * size_z : (a + 1) * size_z, r * 128 : (r + 1) * 128]
                seen[a, pl.ds(i, 1), :] = jnp.sum(
                    jnp.where(hit, both, 0.0), axis=0, keepdims=True
                )

    tiles = rows // tile_rows
    first_tile = lax.rem(me, rows) // tile_rows

    def gather(t, then=None):
        for a in range(3):
            hi, lo = split_bf16(mom[t][a].T)
            mom_t[a * size_z : (a + 1) * size_z, 0:planes] = hi
            mom_t[a * size_z : (a + 1) * size_z, planes : 2 * planes] = lo

        def turn(n):
            return n if then is None else lax.rem(n + first_tile, tiles)

        def use(n, found, own=False):
            pick(turn(n), found)
            if then is not None:
                then(turn(n), own)

        find(turn(0), found_a)
        find(turn(1), found_b)
        use(0, found_a, True)

        def two(n, _):
            find(turn(2 * n + 2), found_a)
            use(2 * n + 1, found_b)
            find(turn(2 * n + 3), found_b)
            use(2 * n + 2, found_a)
            return 0

        lax.fori_loop(0, tiles // 2 - 1, two, 0)
        use(tiles - 1, found_b)
        if then is None:
            for a in range(3):
                slots[1 + a] = slots[1 + a] + slots[0] * (seen[a] - slots[1 + a])

    def deliver(n, own):
        s = pl.ds(pl.multiple_of(n * tile_rows, tile_rows), tile_rows)
        upper = pl.ds(pl.multiple_of(half_dev + n * tile_rows, tile_rows), tile_rows)
        low = lax.broadcasted_iota(i32, (tile_rows, 128), 1) < 64
        c = slots[0, s, :]
        vx, vy, vz = [
            slots[1 + a, s, :] + c * (seen[a, s, :] - slots[1 + a, s, :]) for a in range(3)
        ]
        send2[0, s, :] = jnp.where(low, vx, pltpu.roll(vy, 64, 1))
        send2[0, upper, :] = jnp.where(low, pltpu.roll(vx, 64, 1), vy)
        send2[1, s, :] = jnp.where(low, vz, 0.0)
        send2[1, upper, :] = jnp.where(low, pltpu.roll(vz, 64, 1), 0.0)
        for r in range(tile_rows):
            for side in range(2):
                c = (side * half_dev + r) // n_width + n * (tile_rows // n_width)
                w = r % n_width

                if own:

                    @pl.when(jnp.logical_or(c != chan, w != width))
                    def _():
                        exchange_send(send2, recv2, 1, c, w)

                else:
                    exchange_send(send2, recv2, 1, c, w)

    def nb(dc, dw):
        return (lax.rem(chan + dc + n_chan, n_chan), lax.rem(width + dw + n_width, n_width))

    inner_x, inner_y = pl.ds(1, size_x), pl.ds(PAD, size_y)
    last_x, last_y = size_x, PAD + size_y - 1
    end_x, end_y = size_x + 1, PAD + size_y

    def halo_copy(t, n):
        g = moved[t % 2]
        parts_list = [
            (g.at[0:5, last_x, inner_y], g.at[0:5, 0, inner_y], nb(1, 0)),
            (g.at[8:13, 1, inner_y], g.at[8:13, end_x, inner_y], nb(-1, 0)),
            (g.at[4:9, inner_x, last_y], g.at[4:9, inner_x, PAD - 1], nb(0, 1)),
            (g.at[12:16, inner_x, PAD], g.at[12:16, inner_x, end_y], nb(0, -1)),
            (g.at[0:1, inner_x, PAD], g.at[0:1, inner_x, end_y], nb(0, -1)),
            (g.at[4, last_x, pl.ds(last_y, 1)], g.at[4, 0, pl.ds(PAD - 1, 1)], nb(1, 1)),
            (g.at[12, 1, pl.ds(PAD, 1)], g.at[12, end_x, pl.ds(end_y, 1)], nb(-1, -1)),
            (g.at[0, last_x, pl.ds(PAD, 1)], g.at[0, 0, pl.ds(end_y, 1)], nb(1, -1)),
            (g.at[8, 1, pl.ds(last_y, 1)], g.at[8, end_x, pl.ds(PAD - 1, 1)], nb(-1, 1)),
        ]
        src, dst, to = parts_list[n]
        return pltpu.make_async_remote_copy(
            src, dst, halo_send.at[t, n], halo_recv.at[t, n], device_id=to, device_id_type=MESH
        )

    def load(t, i, h):
        f = []
        for k in range(19):
            if t == 0:
                f.append(pop[k, i, 8 * h : 8 * h + 8, :])
            elif k in STAY:
                f.append(stayed[(t - 1) % 2][STAY[k], i, 8 * h : 8 * h + 8, :])
            else:
                step_x, step_y, _ = LATTICE[k]
                start = PAD + 8 * h - step_y
                f.append(moved[(t - 1) % 2][SLOT_OF[k], i + 1 - step_x, start : start + 8, :])
        return f

    def step_plane(t):
        def one(i):
            coef = [coef_ref[n] for n in range(51)]
            even_c = [coef[6 * a : 6 * a + 6] for a in range(6)]
            odd_c = [
                [coef[36 + 4 * a : 38 + 4 * a], coef[38 + 4 * a : 40 + 4 * a]] for a in range(3)
            ]
            coefs = (even_c, odd_c, coef[48:51])
            for h in range(size_y // 8):
                f = load(t, i, h)
                at = pl.ds(pl.multiple_of(i * size_y + 8 * h, 8), 8)
                count = fields[0, at, :]
                held = [fields[1 + 3 * (t % 2) + a, at, :] for a in range(3)]
                memory = [fields[7 + t - 1 - s, at, :] for s in range(t)]
                seen_m = [[mom[s][a, at, :] for a in range(3)] for s in range(t)]
                solid = solid_ref[i, 8 * h : 8 * h + 8, :] == 1
                out, m = relax_group(f, (count, held, memory), seen_m, solid, coefs)
                for a in range(3):
                    mom[t][a, at, :] = m[a]
                for k in range(19):
                    value = out[k]
                    if LATTICE[k][2]:
                        value = pltpu.roll(value, LATTICE[k][2] % size_z, 1)
                    if k in STAY:
                        stayed[t % 2][STAY[k], i, 8 * h : 8 * h + 8, :] = value
                    else:
                        moved[t % 2][SLOT_OF[k], i + 1, PAD + 8 * h : PAD + 8 * h + 8, :] = value

        return one

    scatter([1, 2, 3, 0], before=place)
    coup = slots[0]
    keep = 1.0 - coup
    weights[3] = coup * coup
    pop_copy.wait()
    small[4].wait()
    for t in range(STEPS):
        plane = step_plane(t)

        def send_ends():
            for n in (5, 6, 7, 8, 0, 1):
                halo_copy(t, n).start()

        def send_sides():
            for n in (2, 3, 4):
                halo_copy(t, n).start()

        if t < STEPS - 1:
            for a in range(3):
                weights[a] = weights[a] * keep
            if t > 0:
                weights[3] = weights[3] * keep
            odd = (t + 1) % 2
            scatter([1 + 3 * odd, 2 + 3 * odd, 3 + 3 * odd, 7 + t], None, plane, send_ends, send_sides)
        else:

            def one(i, _):
                plane(i)
                return 0

            plane(0)
            plane(size_x - 1)
            send_ends()
            lax.fori_loop(1, size_x - 1, one, 0, unroll=2)
            send_sides()
        if t < STEPS - 1:
            gather(t)
        else:
            gather(t, deliver)
        for n in range(9):
            halo_copy(t, n).wait()

    def finish(i, _):
        for h in range(size_y // 8):
            f = load(STEPS, i, h)
            for k in range(19):
                pop[k, i, 8 * h : 8 * h + 8, :] = f[k]
        return 0

    lax.fori_loop(0, size_x, finish, 0)
    out_copy = pltpu.make_async_copy(pop, out_hbm, out_sem)
    out_copy.start()
    recv2[:, pl.ds(me, 1), :] = send2[:, pl.ds(me, 1), :]
    exchange_wait(send2, recv2, 1)

    back_out[...] = recv2[...]
    out_copy.wait()


def finish_kernel(dims, pop_hbm, back_ref, dest_ref, rank_ref, out_hbm, vel_out, held, sems):
    n_dev, parts = dims
    f32, bf16, i32 = jnp.float32, jnp.bfloat16, jnp.int32
    copies_in = [pltpu.make_async_copy(pop_hbm.at[k], held.at[k], sems.at[0, k]) for k in range(19)]
    copies_out = [
        pltpu.make_async_copy(held.at[k], out_hbm.at[k], sems.at[1, k]) for k in range(19)
    ]
    for copy in copies_in:
        copy.start()
    block = min(1024, parts)
    dev_iota = lax.broadcasted_iota(i32, (n_dev, block), 0)
    cap_iota = lax.broadcasted_iota(i32, (CAP, block), 0).astype(f32)
    back = [split_bf16(back_ref[a].T) for a in range(2)]
    back = jnp.concatenate([back[0][0], back[1][0][0:64], back[0][1], back[1][1][0:64]], axis=0)

    def unpack(b, _):
        s = pl.ds(pl.multiple_of(b * block, block), block)
        hits = jnp.where(dev_iota == dest_ref[:, s], 1.0, 0.0).astype(bf16)
        found = dot_nn(back, hits)
        hit = cap_iota == rank_ref[:, s]
        for a in range(3):
            value = found[64 * a : 64 * a + 64] + found[64 * (a + 3) : 64 * (a + 3) + 64]
            vel_out[a : a + 1, s] = jnp.sum(jnp.where(hit, value, 0.0), axis=0, keepdims=True)
        return 0

    blocks = parts // block
    lax.fori_loop(0, blocks // 4, unpack, 0)
    for arrived, leaving in zip(copies_in, copies_out):
        arrived.wait()
        leaving.start()
    lax.fori_loop(blocks // 4, blocks, unpack, 0)
    for copy in copies_out:
        copy.wait()


def per_device(
    n_chan,
    n_width,
    populations,
    moment_rates,
    solid_flags,
    destination,
    local_cell,
    particle_velocity,
    coupling,
):
    _, size_x, size_y, size_z = populations.shape
    parts = destination.shape[0]
    n_dev = n_chan * n_width
    rows = n_dev * CAP // 128
    planes = size_x * size_y
    f32, bf16 = jnp.float32, jnp.bfloat16
    vmem = pl.BlockSpec(memory_space=pltpu.VMEM)
    chunk = 1024
    tile = min(1024, rows * 128 // 2)
    destination = destination.reshape(1, parts)
    moved, back, ranks = pl.pallas_call(
        functools.partial(kernel, (n_chan, n_width, size_x, size_y, size_z, parts)),
        out_shape=(
            jax.ShapeDtypeStruct(populations.shape, f32),
            jax.ShapeDtypeStruct((2, n_dev, 128), f32),
            jax.ShapeDtypeStruct((1, parts), f32),
        ),
        in_specs=[
            pl.BlockSpec(memory_space=pl.ANY),
            pl.BlockSpec(memory_space=pltpu.SMEM),
        ]
        + [pl.BlockSpec(memory_space=pl.ANY)] * 5,
        out_specs=(pl.BlockSpec(memory_space=pl.ANY), vmem, vmem),
        scratch_shapes=[
            pltpu.VMEM(populations.shape, f32),
            pltpu.VMEM(solid_flags.shape, jnp.int32),
            pltpu.VMEM((1, parts), jnp.int32),
            pltpu.VMEM((1, parts), jnp.int32),
            pltpu.VMEM(particle_velocity.shape, f32),
            pltpu.VMEM((1, parts), f32),
            pltpu.VMEM((16, size_x + 2, size_y + 2 * PAD, size_z), f32),
            pltpu.VMEM((16, size_x + 2, size_y + 2 * PAD, size_z), f32),
            pltpu.VMEM((3, size_x, size_y, size_z), f32),
            pltpu.VMEM((3, size_x, size_y, size_z), f32),
            pltpu.VMEM((n_dev, parts), bf16),
            pltpu.VMEM((10 * CAP, parts), bf16),
            pltpu.VMEM((3, n_dev, 128), f32),
            pltpu.VMEM((3, n_dev, 128), f32),
            pltpu.VMEM((2, n_dev, 128), f32),
            pltpu.VMEM((2, n_dev, 128), f32),
            pltpu.VMEM((4, rows, 128), f32),
            pltpu.VMEM((2, rows, 128), f32),
            pltpu.VMEM((4, rows, 128), f32),
            pltpu.VMEM((3, rows, 128), f32),
            pltpu.VMEM((2 * planes, rows * 128), bf16),
            pltpu.VMEM((rows * 128, planes), bf16),
            pltpu.VMEM((size_z, rows * 128), bf16),
            pltpu.VMEM((PIECES, 8 * size_z, chunk), bf16),
            pltpu.VMEM((8 * size_z, planes), f32),
            pltpu.VMEM((3 * size_z, tile), f32),
            pltpu.VMEM((3 * size_z, tile), f32),
            pltpu.VMEM((10, planes, size_z), f32),
            pltpu.VMEM((3, planes, size_z), f32),
            pltpu.VMEM((3, planes, size_z), f32),
            pltpu.VMEM((3, planes, size_z), f32),
            pltpu.VMEM((3, planes, size_z), f32),
            pltpu.VMEM((3 * size_z, 2 * planes), bf16),
            pltpu.VMEM((51, 8, 128), f32),
            pltpu.SemaphoreType.DMA,
            pltpu.SemaphoreType.DMA((5,)),
            pltpu.SemaphoreType.DMA,
            pltpu.SemaphoreType.DMA((2,)),
            pltpu.SemaphoreType.DMA((2,)),
            pltpu.SemaphoreType.DMA((STEPS, 9)),
            pltpu.SemaphoreType.DMA((STEPS, 9)),
        ],
        compiler_params=pltpu.CompilerParams(
            collective_id=0, has_side_effects=True, vmem_limit_bytes=56 * 1024 * 1024
        ),
        name="lattice_steps",
    )(
        populations,
        moment_rates,
        solid_flags,
        destination,
        local_cell.reshape(1, parts),
        particle_velocity,
        coupling.reshape(1, parts),
    )
    return pl.pallas_call(
        functools.partial(finish_kernel, (n_dev, parts)),
        out_shape=(
            jax.ShapeDtypeStruct(populations.shape, f32),
            jax.ShapeDtypeStruct(particle_velocity.shape, f32),
        ),
        in_specs=[pl.BlockSpec(memory_space=pl.ANY), vmem, vmem, vmem],
        out_specs=(pl.BlockSpec(memory_space=pl.ANY), vmem),
        scratch_shapes=[
            pltpu.VMEM(populations.shape, f32),
            pltpu.SemaphoreType.DMA((2, 19)),
        ],
        compiler_params=pltpu.CompilerParams(vmem_limit_bytes=56 * 1024 * 1024),
        name="particles_back",
    )(moved, back, destination, ranks)


def solution(mesh):
    return jax.shard_map(
        functools.partial(per_device, mesh.shape["chan"], mesh.shape["width"]),
        mesh=mesh,
        in_specs=(
            P(None, "chan", "width", None),
            P(),
            P("chan", "width", None),
            P(("chan", "width"), None),
            P(("chan", "width")),
            P(None, ("chan", "width")),
            P(("chan", "width")),
        ),
        out_specs=(P(None, "chan", "width", None), P(None, ("chan", "width"))),
        check_vma=False,
    )
```
